32 devices in a mesh: ctx: 16 (over z, x, core), ch: 2 (over y).
Axes of the slice: x: 2, y: 2, z: 4, core: 2. Of those that a mesh axis runs over, the one named last changes fastest.
Arguments:
- saved_input: bfloat16 [16, 16, 49152], P(None, 'ch', 'ctx'), may hold values from -6 to 6
- out_grad: bfloat16 [16, 16, 49152], P(None, 'ch', 'ctx'), may hold values from -6 to 6
- block_offsets: int32 [16], replicated, may hold values from 1 to 359, as said below
- head_len: int32 [1], replicated, may hold values from 16 to 128
Outputs:
- grad_filter: float32 [16, 2176], P(None, 'ctx')
The draws below stay inside these ranges and needn't reach their ends.
Inputs may be any that keep to these rules, and one draw needn't show every extreme that they name: `block_offsets`: 16 distinct values; the largest is 359.
All inputs are finite; a program needn't handle non-finite values.
Results may differ from the reference program's by a relative error of at most 0.0003.
Values may be sent and summed in bfloat16 or wider, within the bound.
A program may use at most 64 MiB of HBM per device.

```python
import math
import jax
import jax.numpy as jnp
from jax import lax

GSIZE = 16
FILT = 16
NBLK = 16
TOKENS = 49152
LAGTILES = 360


def draw_block_offsets(key, part):
    first_key, second_key = jax.random.split(jax.random.fold_in(key, 11))
    picked = jax.random.permutation(first_key, LAGTILES - 2)[:NBLK - 1] + 1
    listed = jnp.concatenate([picked, jnp.full((1,), LAGTILES - 1)]).astype(jnp.int32)
    return jax.random.permutation(second_key, listed)


def steps_of(own_key, shape, cuts, least, top_value):
    loudness, own = 1.0, jax.random.fold_in(own_key, 6)
    for position, shards_of in cuts:
        heights = jnp.exp(jax.random.uniform(jax.random.fold_in(own, position), (shards_of,), jnp.float32, least / len(cuts), top_value / len(cuts)))
        loudness = loudness * jnp.repeat(heights, shape[position] // shards_of).reshape([-1 if axis == position else 1 for axis in range(len(shape))])
    return loudness


def noise(rng, dims, scale, most, shards=(), kind=jnp.bfloat16):
    values = scale * jax.random.normal(rng, dims, jnp.float32)
    if shards:
        values = values * steps_of(rng, dims, shards, -0.22, 0.18)
    return jnp.clip(values, -most, most).astype(kind)


def setup_inputs(seed: int = 0) -> dict:
    keys = jax.random.split(jax.random.key(seed), 5)
    saved_input = noise(keys[0], (FILT, GSIZE, TOKENS), 1.0, 6.0, ((1, 2), (2, 16)))
    out_grad = noise(keys[1], (FILT, GSIZE, TOKENS), 1.0, 6.0, ((1, 2), (2, 16)))
    block_offsets = draw_block_offsets(jax.random.fold_in(keys[4], 71), 0)
    head_len = jax.random.randint(keys[3], (1,), 16, 129).astype(jnp.int32)
    return dict(saved_input=saved_input, out_grad=out_grad, block_offsets=block_offsets, head_len=head_len)


def diagonals(lag_grid):
    flipped = lag_grid[:, ::-1]
    diag_band = flipped.reshape(-1)[127:127 + 255 * 128].reshape(128, 255)[:, :128]
    return lax.optimization_barrier(jnp.sum(diag_band, axis=0))

def reference(saved_input, out_grad, block_offsets, head_len):
    tile_count = TOKENS // 128
    pad_width = (LAGTILES + 1) * 128
    offsets = jnp.concatenate([jnp.zeros((1,), jnp.int32), block_offsets.astype(jnp.int32)])

    def per_filter(filter_item):
        input_rows, grad_part = filter_item
        padded_x = jnp.concatenate([jnp.zeros((GSIZE, pad_width), jnp.float32), input_rows.astype(jnp.float32)], axis=1)
        grad_rows = grad_part.astype(jnp.float32).reshape(GSIZE, tile_count, 128)

        def per_block(offset):
            slice_start = (pad_width - (offset + 1) * 128).astype(jnp.int32)
            window_span = lax.dynamic_slice_in_dim(padded_x, slice_start, (tile_count + 1) * 128, 1)
            left_tiles = window_span[:, :tile_count * 128].reshape(GSIZE, tile_count, 128)
            right_tiles = window_span[:, 128:].reshape(GSIZE, tile_count, 128)
            window = jnp.concatenate([left_tiles, right_tiles], axis=2)
            lag_grid = jnp.einsum('gai,gak->ik', grad_rows, window, precision=lax.Precision.HIGHEST)
            return diagonals(lag_grid)
        return lax.map(per_block, offsets).reshape(-1)
    lag_sums = lax.map(per_filter, (saved_input, out_grad))
    lag_index = lax.broadcasted_iota(jnp.int32, (1, (NBLK + 1) * 128), 1)
    keep_mask = (lag_index >= 128) | (lag_index < head_len[0])
    loss_scale = 1.0 / math.sqrt(TOKENS * GSIZE)
    return jnp.where(keep_mask, lag_sums, jnp.zeros_like(lag_sums)) * loss_scale
```

```python
import functools
import math

import jax
import jax.numpy as jnp
from jax import lax
from jax.experimental import pallas as pl
from jax.experimental.pallas import tpu as pltpu
from jax.sharding import PartitionSpec as P

LAYERS = 4
MESH = pl.DeviceIdType.MESH


def kernel(
    ctx_count, ch_count, copies,
    off_ref, x_ref, dy_ref, out_ref,
    pbuf, qbuf, q2buf, wide, qt, sums, lags, parts, joined,
    own_sem, psem, qsem, outer_sem, opp_sem, psend, qsend, fsend, osend, xsend, xrecv,
):
    filters, rows, _ = x_ref.shape
    blocks = lags.shape[0]
    depth = ctx_count // LAYERS
    mine = filters // depth
    half = mine // 2
    layer_rows = depth * rows
    ch_rows = 16 // copies
    groups = wide.shape[0] // copies
    tiles = layer_rows // ch_rows
    base = tiles + copies
    piece = out_ref.shape[1]
    total = ctx_count * ch_count

    ctx = lax.axis_index("ctx")
    ch = lax.axis_index("ch")
    me = ctx * ch_count + ch
    layer, pos = ctx // depth, ctx % depth
    up = layer // 2
    own = layer % 2
    center = own != up
    outer = own == up

    barrier = pltpu.get_barrier_semaphore()

    def greet(step, carry):
        to = (me + step) % total
        pl.semaphore_signal(
            barrier, inc=1, device_id=(to // ch_count, to % ch_count), device_id_type=MESH
        )
        return carry

    lax.fori_loop(1, total, greet, 0)
    pl.semaphore_wait(barrier, total - 1)

    def start_layer(src, dst_of, sem, send_sem, own_idx, q):
        filt = (q + up * half) % mine
        pltpu.make_async_copy(src.at[pos * mine + filt], dst_of(pos), own_sem.at[own_idx, q]).start()
        for step in range(1, depth):
            peer = (pos + step) % depth
            pltpu.make_async_remote_copy(
                src_ref=src.at[peer * mine + filt],
                dst_ref=dst_of(pos),
                send_sem=send_sem.at[q],
                recv_sem=sem.at[q],
                device_id=(layer * depth + peer, ch),
                device_id_type=MESH,
            ).start()

    order = list(range(half, mine)) + list(range(half))

    def start_all(p_src, q_src):
        for q in order:
            start_layer(p_src, lambda at: pbuf.at[q, own, at], psem, psend, 0, q)
        for q in order:
            start_layer(q_src, lambda at: qbuf.at[q, at], qsem, qsend, 1, q)

    @pl.when(up == 0)
    def _():
        start_all(x_ref, dy_ref)

    @pl.when(up == 1)
    def _():
        start_all(dy_ref, x_ref)

    def drain(ref, sem):
        pltpu.make_async_copy(ref, ref, sem).wait()

    wide[...] = jnp.zeros_like(wide)

    @pl.when(outer)
    def _():
        pbuf[:, 1 - own] = jnp.zeros(pbuf.shape[:1] + pbuf.shape[2:], pbuf.dtype)

    for q in order:
        drain(pbuf.at[q, own, 0], own_sem.at[0, q])
        drain(pbuf.at[q, own, pl.ds(0, depth - 1)], psem.at[q])

        @pl.when(outer)
        def _():
            pltpu.make_async_remote_copy(
                src_ref=pbuf.at[q, own],
                dst_ref=pbuf.at[q, own],
                send_sem=fsend.at[q],
                recv_sem=outer_sem.at[q],
                device_id=((1 + up) * depth + pos, ch),
                device_id_type=MESH,
            ).start()

        def pass_on(which):
            pltpu.make_async_remote_copy(
                src_ref=pbuf.at[q, which],
                dst_ref=q2buf.at[q - half, which],
                send_sem=osend.at[q - half, which],
                recv_sem=opp_sem.at[q - half, which],
                device_id=((2 - up) * depth + pos, ch),
                device_id_type=MESH,
            ).start()

        if q >= half:

            @pl.when(center)
            def _():
                pass_on(own)

    for q in range(half, mine):

        @pl.when(center)
        def _():
            drain(pbuf.at[q, 1 - own], outer_sem.at[q])
            pltpu.make_async_remote_copy(
                src_ref=pbuf.at[q, 1 - own],
                dst_ref=q2buf.at[q - half, 1 - own],
                send_sem=osend.at[q - half, 1 - own],
                recv_sem=opp_sem.at[q - half, 1 - own],
                device_id=((2 - up) * depth + pos, ch),
                device_id_type=MESH,
            ).start()

    row = lax.broadcasted_iota(jnp.int32, (128, 128), 0)
    col = lax.broadcasted_iota(jnp.int32, (128, 128), 1)
    eye = (row == col).astype(jnp.bfloat16)
    first = row >= col + up

    def turn(block):
        return lax.dot_general(
            eye, block, (((1,), (1,)), ((), ())), preferred_element_type=jnp.float32
        ).astype(jnp.bfloat16)

    def offset_of(k):
        return off_ref[lax.max(k - 1, 0)] * lax.min(k, 1)

    def window(q_layer, offset):
        start = (q_layer - 2 * up) * tiles + (2 * up - 1) * offset + up
        start = lax.min(lax.max(start, -tiles), 2 * tiles + 1) + base
        at = lax.rem(start, copies) * groups + lax.div(start, copies)
        return jnp.concatenate([wide[at + step] for step in range(layer_rows // 16)], axis=0)

    def folded(grid):
        picked = jnp.where(first, grid[:, :128], grid[:, 128:])
        acc = picked[0:8]
        for b in range(1, 16):
            acc = acc + pltpu.roll(picked[8 * b : 8 * b + 8], 128 - 8 * b, 1)
        return acc

    def dot(left, right):
        return jnp.dot(left, right, preferred_element_type=jnp.float32)

    for q in order:
        filt = (q + up * half) % mine
        if q < half:

            @pl.when(center)
            def _():
                drain(pbuf.at[q, 1 - own], outer_sem.at[q])

        pad = jnp.zeros((16, 128), jnp.float32)
        flat = pbuf[q].reshape(2 * layer_rows, 128).astype(jnp.float32)
        flat = jnp.concatenate([pad, flat, pad], axis=0)
        long = 2 * layer_rows + 32
        for move in range(-1, copies):
            moved = flat if move == 0 else pltpu.roll(flat, (-move * ch_rows) % long, 0)
            moved = moved.astype(jnp.bfloat16).reshape(long // 16, 16, 128)
            for side in range(2):
                if 0 <= move + side < copies:
                    lo = (move + side) * groups + base * ch_rows // 16 - 1
                    wide[lo : lo + long // 16, :, side * 128 : side * 128 + 128] = moved
        drain(qbuf.at[q, 0], own_sem.at[1, q])
        drain(qbuf.at[q, pl.ds(0, depth - 1)], qsem.at[q])
        qt[0] = turn(qbuf[q].reshape(layer_rows, 128))

        def own_block(k, carry):
            sums[k, filt] = folded(dot(qt[0], window(layer, offset_of(k))))
            return carry

        lax.fori_loop(0, blocks, own_block, 0)

        if q < half:

            @pl.when(center)
            def _():
                for which in range(2):
                    drain(q2buf.at[q, which], opp_sem.at[q, which])
                    qt[which] = turn(q2buf[q, which].reshape(layer_rows, 128))

                def far_block(k, carry):
                    offset = offset_of(k)
                    far = 2 - 2 * up
                    grid = dot(qt[0], window(far, offset)) + dot(qt[1], window(far + 1, offset))
                    sums[k, filt] = sums[k, filt] + folded(grid)
                    return carry

                lax.fori_loop(0, blocks, far_block, 0)

    rolled = sums[...].reshape(blocks * mine * 8, 128)
    small = lax.broadcasted_iota(jnp.int32, rolled.shape, 0)
    for bit in (1, 2, 4):
        rolled = jnp.where((small & bit) != 0, pltpu.roll(rolled, 128 - bit, 1), rolled)
    summed = jnp.sum(rolled.reshape(blocks * mine, 8, 128), axis=1)
    flip = (128 - col) % 128
    order_mat = (row == jnp.where(up == 1, col, flip)).astype(jnp.float32)
    summed = jnp.dot(
        summed, order_mat, precision=lax.Precision.HIGHEST, preferred_element_type=jnp.float32
    )
    for k in range(blocks):
        lags[k] = summed[k * mine : (k + 1) * mine]

    def first_row(at):
        return jnp.minimum((at * piece) // 128, blocks - 2)

    def hand_out(step, carry):
        to = (me + step) % total
        pltpu.make_async_remote_copy(
            src_ref=lags.at[pl.ds(first_row(to // ch_count), 2)],
            dst_ref=parts.at[me],
            send_sem=xsend,
            recv_sem=xrecv,
            device_id=(to // ch_count, to % ch_count),
            device_id_type=MESH,
        ).start()
        return carry

    lax.fori_loop(1, total, hand_out, 0)
    start_row = first_row(ctx)
    parts[me] = lags[pl.ds(start_row, 2)]
    drain(parts.at[pl.ds(0, total - 1)], xrecv)
    for at in range(depth):
        acc = None
        for lay in range(LAYERS):
            for h in range(ch_count):
                term = parts[(lay * depth + at) * ch_count + h]
                acc = term if acc is None else acc + term
        joined[at * mine : (at + 1) * mine, 0:128] = acc[0]
        joined[at * mine : (at + 1) * mine, 128:256] = acc[1]
    skip = ctx * piece - start_row * 128
    out_ref[...] = pltpu.roll(joined[...], lax.rem(256 - skip, 256), 1)[:, :piece]

    drain(parts.at[pl.ds(0, total - 1)], xsend)
    for q in range(mine):
        drain(pbuf.at[q, 0, pl.ds(0, depth - 1)], psend.at[q])
        drain(qbuf.at[q, pl.ds(0, depth - 1)], qsend.at[q])

    @pl.when(outer)
    def _():
        for q in range(mine):
            drain(pbuf.at[q, 0], fsend.at[q])

    @pl.when(center)
    def _():
        for q in range(half):
            for which in range(2):
                drain(pbuf.at[q, 0], osend.at[q, which])


def local(ctx_count, ch_count, saved_input, out_grad, block_offsets, head_len):
    filters, local_ch, tok_dev = saved_input.shape
    tile_count = tok_dev // 128
    rows = tile_count * local_ch
    blocks = block_offsets.shape[0] + 1
    depth = ctx_count // LAYERS
    mine = filters // depth
    half = mine // 2
    copies = 16 // local_ch
    layer_rows = depth * rows
    piece = blocks * 128 // ctx_count
    total = ctx_count * ch_count
    loss_scale = 1.0 / math.sqrt(tok_dev * ctx_count * local_ch * ch_count)

    def tiled(array):
        split = array.reshape(filters, local_ch, tile_count, 128)
        return jnp.transpose(split, (0, 2, 1, 3)).reshape(filters, rows, 128)

    bf16, f32 = jnp.bfloat16, jnp.float32
    dma = pltpu.SemaphoreType.DMA
    taps = pl.pallas_call(
        functools.partial(kernel, ctx_count, ch_count, copies),
        out_shape=jax.ShapeDtypeStruct((filters, piece), f32),
        in_specs=[pl.BlockSpec(memory_space=pltpu.SMEM)] + [pl.BlockSpec(memory_space=pl.ANY)] * 2,
        out_specs=pl.BlockSpec(memory_space=pltpu.VMEM),
        scratch_shapes=[
            pltpu.VMEM((mine, 2, depth, rows, 128), bf16),
            pltpu.VMEM((mine, depth, rows, 128), bf16),
            pltpu.VMEM((half, 2, depth, rows, 128), bf16),
            pltpu.VMEM((copies * (layer_rows // 4 + 4), 16, 256), bf16),
            pltpu.VMEM((2, 128, layer_rows), bf16),
            pltpu.VMEM((blocks, mine, 8, 128), f32),
            pltpu.VMEM((blocks, mine, 128), f32),
            pltpu.VMEM((total, 2, mine, 128), f32),
            pltpu.VMEM((filters, 256), f32),
            dma((2, mine)),
            dma((mine,)),
            dma((mine,)),
            dma((mine,)),
            dma((half, 2)),
            dma((mine,)),
            dma((mine,)),
            dma((mine,)),
            dma((half, 2)),
            dma,
            dma,
        ],
        compiler_params=pltpu.CompilerParams(
            collective_id=0, has_side_effects=True, vmem_limit_bytes=48 * 1024 * 1024
        ),
        cost_estimate=pl.CostEstimate(flops=7 * 10**9, bytes_accessed=4 * 10**6, transcendentals=0),
    )(block_offsets, tiled(saved_input), tiled(out_grad))
    lag = lax.broadcasted_iota(jnp.int32, taps.shape, 1) + lax.axis_index("ctx") * piece
    keep = (lag >= 128) | (lag < head_len[0])
    return jnp.where(keep, taps * loss_scale, jnp.zeros_like(taps))


def solution(mesh):
    ctx_count, ch_count = mesh.shape["ctx"], mesh.shape["ch"]
    in_specs = (P(None, "ch", "ctx"), P(None, "ch", "ctx"), P(), P())
    out_specs = P(None, "ctx")
    return jax.shard_map(
        functools.partial(local, ctx_count, ch_count),
        mesh=mesh, in_specs=in_specs, out_specs=out_specs, check_vma=False,
    )
```

```python
import functools
import math

import jax
import jax.numpy as jnp
from jax import lax
from jax.experimental import pallas as pl
from jax.experimental.pallas import tpu as pltpu
from jax.sharding import PartitionSpec as P

LAYERS = 4
MESH = pl.DeviceIdType.MESH


def kernel(
    ctx_count, ch_count, copies,
    off_ref, x_ref, dy_ref, out_ref,
    pbuf, qbuf, q2buf, wide, sums, lags, parts, joined,
    own_sem, psem, qsem, outer_sem, opp_sem, psend, qsend, fsend, osend, xsend, xrecv,
):
    filters, pieces = x_ref.shape[:2]
    blocks = lags.shape[0]
    depth = ctx_count // LAYERS
    mine = filters // depth
    half = mine // 2
    layer_rows = depth * pieces * 16
    ch_rows = 16 // copies
    groups = pbuf.shape[1]
    tiles = layer_rows // ch_rows
    base = tiles + copies
    lead = base // copies
    piece = out_ref.shape[1]
    total = ctx_count * ch_count

    ctx = lax.axis_index("ctx")
    ch = lax.axis_index("ch")
    me = ctx * ch_count + ch
    layer, pos = ctx // depth, ctx % depth
    up = layer // 2
    own = layer % 2
    center = own != up
    outer = own == up

    barrier = pltpu.get_barrier_semaphore()

    def greet(step, carry):
        to = (me + step) % total
        pl.semaphore_signal(
            barrier, inc=1, device_id=(to // ch_count, to % ch_count), device_id_type=MESH
        )
        return carry

    lax.fori_loop(1, total, greet, 0)
    pl.semaphore_wait(barrier, total - 1)

    def start_layer(src, dst_of, sem, send_sem, own_idx, q):
        filt = (q + up * half) % mine
        pltpu.make_async_copy(src.at[pos * mine + filt], dst_of(pos), own_sem.at[own_idx, q]).start()
        for step in range(1, depth):
            peer = (pos + step) % depth
            pltpu.make_async_remote_copy(
                src_ref=src.at[peer * mine + filt],
                dst_ref=dst_of(pos),
                send_sem=send_sem.at[q],
                recv_sem=sem.at[q],
                device_id=(layer * depth + peer, ch),
                device_id_type=MESH,
            ).start()

    order = list(range(half, mine)) + list(range(half))

    def landed(q, which, at=0, count=depth):
        return pbuf.at[q, pl.ds(lead + (which * depth + at) * pieces, count * pieces)]

    def start_all(p_src, q_src):
        for q in order:
            start_layer(p_src, lambda at: landed(q, own, at, 1), psem, psend, 0, q)
        for q in order:
            start_layer(q_src, lambda at: qbuf.at[q, at], qsem, qsend, 1, q)

    @pl.when(up == 0)
    def _():
        start_all(x_ref, dy_ref)

    @pl.when(up == 1)
    def _():
        start_all(dy_ref, x_ref)

    def drain(ref, sem):
        pltpu.make_async_copy(ref, ref, sem).wait()

    pbuf[:, 0:lead] = jnp.zeros((mine, lead, 16, 128), pbuf.dtype)
    tail = lead + 2 * depth * pieces
    pbuf[:, tail:groups] = jnp.zeros((mine, groups - tail, 16, 128), pbuf.dtype)
    if copies > 1:
        wide[...] = jnp.zeros_like(wide)

    @pl.when(outer)
    def _():
        pbuf[:, pl.ds(lead + (1 - own) * depth * pieces, depth * pieces)] = jnp.zeros(
            (mine, depth * pieces, 16, 128), pbuf.dtype
        )

    def pass_on(q, which):
        pltpu.make_async_remote_copy(
            src_ref=landed(q, which),
            dst_ref=q2buf.at[q - half, which],
            send_sem=osend.at[q - half, which],
            recv_sem=opp_sem.at[q - half, which],
            device_id=((2 - up) * depth + pos, ch),
            device_id_type=MESH,
        ).start()

    for q in order:
        drain(landed(q, own, 0, 1), own_sem.at[0, q])
        drain(landed(q, own, 0, depth - 1), psem.at[q])

        @pl.when(outer)
        def _():
            pltpu.make_async_remote_copy(
                src_ref=landed(q, own),
                dst_ref=landed(q, own),
                send_sem=fsend.at[q],
                recv_sem=outer_sem.at[q],
                device_id=((1 + up) * depth + pos, ch),
                device_id_type=MESH,
            ).start()

        if q >= half:

            @pl.when(center)
            def _():
                pass_on(q, own)

    for q in range(half, mine):

        @pl.when(center)
        def _():
            drain(landed(q, 1 - own), outer_sem.at[q])
            pass_on(q, 1 - own)

    row = lax.broadcasted_iota(jnp.int32, (128, 128), 0)
    col = lax.broadcasted_iota(jnp.int32, (128, 128), 1)
    eye = (row == col).astype(jnp.bfloat16)
    first = row >= col + up

    def turn(block):
        return lax.dot_general(
            eye, block, (((1,), (1,)), ((), ())), preferred_element_type=jnp.float32
        ).astype(jnp.bfloat16)

    def offset_of(k):
        return off_ref[k - 1] if k else 0

    def rows_from(q, start):
        at = lax.div(start, copies)
        which = lax.rem(start, copies)
        steps = range(layer_rows // 16)
        if copies == 1:
            return jnp.concatenate([pbuf[q, at + step] for step in steps], axis=0)
        return jnp.concatenate([wide[which * groups + at + step] for step in steps], axis=0)

    def window(q, q_layer, offset):
        start = (q_layer - 2 * up) * tiles + (2 * up - 1) * offset + up
        start = lax.min(lax.max(start, -tiles), 2 * tiles + 1) + base
        return jnp.concatenate([rows_from(q, start), rows_from(q, start - 1)], axis=1)

    def folded(grid):
        picked = jnp.where(first, grid[:, :128], grid[:, 128:])
        acc = picked[0:8]
        for b in range(1, 16):
            acc = acc + pltpu.roll(picked[8 * b : 8 * b + 8], 128 - 8 * b, 1)
        return acc

    def dot(left, right):
        return jnp.dot(left, right, preferred_element_type=jnp.float32)

    def work(index, carry):
        q = lax.rem(index + half, mine)
        filt = lax.rem(q + up * half, mine)

        @pl.when(center & (q < half))
        def _():
            drain(landed(q, 1 - own), outer_sem.at[q])

        lo, count = lead - 1, 2 * depth * pieces + 2
        if copies > 1:
            near = pbuf[q, lo : lo + count]
            wide[lo : lo + count] = near
            flat = near.astype(jnp.float32).reshape(count * 16, 128)
            for move in range(1, copies):
                moved = pltpu.roll(flat, count * 16 - move * ch_rows, 0).astype(jnp.bfloat16)
                wide[move * groups + lo : move * groups + lo + count] = moved.reshape(count, 16, 128)
        drain(qbuf.at[q, 0], own_sem.at[1, q])
        drain(qbuf.at[q, pl.ds(0, depth - 1)], qsem.at[q])
        turned = turn(qbuf[q].reshape(layer_rows, 128))
        for k in range(blocks):
            sums[k, filt] = folded(dot(turned, window(q, layer, offset_of(k))))

        @pl.when(center & (q < half))
        def _():
            for which in range(2):
                drain(q2buf.at[q, which], opp_sem.at[q, which])
            left = turn(q2buf[q, 0].reshape(layer_rows, 128))
            right = turn(q2buf[q, 1].reshape(layer_rows, 128))
            far = 2 - 2 * up
            for k in range(blocks):
                grid = dot(left, window(q, far, offset_of(k)))
                grid = grid + dot(right, window(q, far + 1, offset_of(k)))
                sums[k, filt] = sums[k, filt] + folded(grid)

        return carry

    lax.fori_loop(0, mine, work, 0)

    rolled = sums[...].reshape(blocks * mine * 8, 128)
    small = lax.broadcasted_iota(jnp.int32, rolled.shape, 0)
    for bit in (1, 2, 4):
        rolled = jnp.where((small & bit) != 0, pltpu.roll(rolled, 128 - bit, 1), rolled)
    summed = jnp.sum(rolled.reshape(blocks * mine, 8, 128), axis=1)
    flip = (128 - col) % 128
    order_mat = (row == jnp.where(up == 1, col, flip)).astype(jnp.float32)
    summed = jnp.dot(
        summed, order_mat, precision=lax.Precision.HIGHEST, preferred_element_type=jnp.float32
    )
    for k in range(blocks):
        lags[k] = summed[k * mine : (k + 1) * mine]

    def first_row(at):
        return jnp.minimum((at * piece) // 128, blocks - 2)

    def hand_out(step, carry):
        to = (me + step) % total
        pltpu.make_async_remote_copy(
            src_ref=lags.at[pl.ds(first_row(to // ch_count), 2)],
            dst_ref=parts.at[me],
            send_sem=xsend,
            recv_sem=xrecv,
            device_id=(to // ch_count, to % ch_count),
            device_id_type=MESH,
        ).start()
        return carry

    lax.fori_loop(1, total, hand_out, 0)
    start_row = first_row(ctx)
    parts[me] = lags[pl.ds(start_row, 2)]
    drain(parts.at[pl.ds(0, total - 1)], xrecv)
    for at in range(depth):
        acc = None
        for lay in range(LAYERS):
            for h in range(ch_count):
                term = parts[(lay * depth + at) * ch_count + h]
                acc = term if acc is None else acc + term
        joined[at * mine : (at + 1) * mine, 0:128] = acc[0]
        joined[at * mine : (at + 1) * mine, 128:256] = acc[1]
    skip = ctx * piece - start_row * 128
    out_ref[...] = pltpu.roll(joined[...], lax.rem(256 - skip, 256), 1)[:, :piece]

    drain(parts.at[pl.ds(0, total - 1)], xsend)
    for q in range(mine):
        drain(landed(q, 0, 0, depth - 1), psend.at[q])
        drain(qbuf.at[q, pl.ds(0, depth - 1)], qsend.at[q])

    @pl.when(outer)
    def _():
        for q in range(mine):
            drain(landed(q, 0), fsend.at[q])

    @pl.when(center)
    def _():
        for q in range(half):
            for which in range(2):
                drain(landed(q, 0), osend.at[q, which])


def local(ctx_count, ch_count, saved_input, out_grad, block_offsets, head_len):
    filters, local_ch, tok_dev = saved_input.shape
    tile_count = tok_dev // 128
    rows = tile_count * local_ch
    blocks = block_offsets.shape[0] + 1
    depth = ctx_count // LAYERS
    mine = filters // depth
    half = mine // 2
    copies = 16 // local_ch
    pieces = rows // 16
    groups = 4 * depth * pieces + 4
    piece = blocks * 128 // ctx_count
    total = ctx_count * ch_count
    loss_scale = 1.0 / math.sqrt(tok_dev * ctx_count * local_ch * ch_count)

    def tiled(array):
        split = array.reshape(filters, local_ch, tile_count, 128)
        return jnp.transpose(split, (0, 2, 1, 3)).reshape(filters, pieces, 16, 128)

    bf16, f32 = jnp.bfloat16, jnp.float32
    dma = pltpu.SemaphoreType.DMA
    taps = pl.pallas_call(
        functools.partial(kernel, ctx_count, ch_count, copies),
        out_shape=jax.ShapeDtypeStruct((filters, piece), f32),
        in_specs=[pl.BlockSpec(memory_space=pltpu.SMEM)] + [pl.BlockSpec(memory_space=pl.ANY)] * 2,
        out_specs=pl.BlockSpec(memory_space=pltpu.VMEM),
        scratch_shapes=[
            pltpu.VMEM((mine, groups, 16, 128), bf16),
            pltpu.VMEM((mine, depth, pieces, 16, 128), bf16),
            pltpu.VMEM((half, 2, depth * pieces, 16, 128), bf16),
            pltpu.VMEM((copies * groups, 16, 128), bf16),
            pltpu.VMEM((blocks, mine, 8, 128), f32),
            pltpu.VMEM((blocks, mine, 128), f32),
            pltpu.VMEM((total, 2, mine, 128), f32),
            pltpu.VMEM((filters, 256), f32),
            dma((2, mine)),
            dma((mine,)),
            dma((mine,)),
            dma((mine,)),
            dma((half, 2)),
            dma((mine,)),
            dma((mine,)),
            dma((mine,)),
            dma((half, 2)),
            dma,
            dma,
        ],
        compiler_params=pltpu.CompilerParams(
            collective_id=0, has_side_effects=True, vmem_limit_bytes=60 * 1024 * 1024
        ),
        cost_estimate=pl.CostEstimate(flops=7 * 10**9, bytes_accessed=4 * 10**6, transcendentals=0),
    )(block_offsets, tiled(saved_input), tiled(out_grad))
    lag = lax.broadcasted_iota(jnp.int32, taps.shape, 1) + lax.axis_index("ctx") * piece
    keep = (lag >= 128) | (lag < head_len[0])
    return jnp.where(keep, taps * loss_scale, jnp.zeros_like(taps))


def solution(mesh):
    ctx_count, ch_count = mesh.shape["ctx"], mesh.shape["ch"]
    in_specs = (P(None, "ch", "ctx"), P(None, "ch", "ctx"), P(), P())
    out_specs = P(None, "ctx")
    return jax.shard_map(
        functools.partial(local, ctx_count, ch_count),
        mesh=mesh, in_specs=in_specs, out_specs=out_specs, check_vma=False,
    )
```

```python
import functools
import math

import jax
import jax.numpy as jnp
from jax import lax
from jax.experimental import pallas as pl
from jax.experimental.pallas import tpu as pltpu
from jax.sharding import PartitionSpec as P

LAYERS = 4
MESH = pl.DeviceIdType.MESH


def kernel(
    ctx_count, ch_count, copies,
    off_ref, x_ref, dy_ref, out_ref,
    pbuf, qbuf, q2buf, wide, sums, lags, parts, joined,
    own_sem, psem, qsem, outer_sem, opp_sem, psend, qsend, fsend, osend, xsend, xrecv,
):
    filters, pieces = x_ref.shape[:2]
    blocks = lags.shape[0]
    depth = ctx_count // LAYERS
    mine = filters // depth
    half = mine // 2
    layer_rows = depth * pieces * 16
    ch_rows = 16 // copies
    groups = pbuf.shape[1]
    tiles = layer_rows // ch_rows
    base = tiles + copies
    lead = base // copies
    piece = out_ref.shape[1]
    total = ctx_count * ch_count

    ctx = lax.axis_index("ctx")
    ch = lax.axis_index("ch")
    me = ctx * ch_count + ch
    layer, pos = ctx // depth, ctx % depth
    up = layer // 2
    own = layer % 2
    center = own != up
    outer = own == up

    barrier = pltpu.get_barrier_semaphore()

    def greet(step, carry):
        to = lax.rem(me + step, total)
        pl.semaphore_signal(
            barrier, inc=1, device_id=(to // ch_count, to % ch_count), device_id_type=MESH
        )
        return carry

    lax.fori_loop(1, total, greet, 0)

    def landed(q, which, at=0, count=depth):
        return pbuf.at[q, pl.ds(lead + (which * depth + at) * pieces, count * pieces)]

    def drain(ref, sem):
        pltpu.make_async_copy(ref, ref, sem).wait()

    pbuf[:, 0:lead] = jnp.zeros((mine, lead, 16, 128), pbuf.dtype)
    tail = lead + 2 * depth * pieces
    pbuf[:, tail:groups] = jnp.zeros((mine, groups - tail, 16, 128), pbuf.dtype)
    if copies > 1:
        wide[...] = jnp.zeros_like(wide)

    @pl.when(outer)
    def _():
        pbuf[:, pl.ds(lead + (1 - own) * depth * pieces, depth * pieces)] = jnp.zeros(
            (mine, depth * pieces, 16, 128), pbuf.dtype
        )

    pl.semaphore_wait(barrier, total - 1)

    def start_layer(src, dst, sem, send_sem, own_idx, q):
        filt = lax.rem(q + up * half, mine)
        pltpu.make_async_copy(src.at[pos * mine + filt], dst, own_sem.at[own_idx, q]).start()
        for step in range(1, depth):
            peer = lax.rem(pos + step, depth)
            pltpu.make_async_remote_copy(
                src_ref=src.at[peer * mine + filt],
                dst_ref=dst,
                send_sem=send_sem.at[q],
                recv_sem=sem.at[q],
                device_id=(layer * depth + peer, ch),
                device_id_type=MESH,
            ).start()

    def start_p(q):
        @pl.when(up == 0)
        def _():
            start_layer(x_ref, landed(q, own, pos, 1), psem, psend, 0, q)

        @pl.when(up == 1)
        def _():
            start_layer(dy_ref, landed(q, own, pos, 1), psem, psend, 0, q)

    def start_q(q):
        @pl.when(up == 0)
        def _():
            start_layer(dy_ref, qbuf.at[q, pos], qsem, qsend, 1, q)

        @pl.when(up == 1)
        def _():
            start_layer(x_ref, qbuf.at[q, pos], qsem, qsend, 1, q)

    def await_q(q):
        drain(qbuf.at[q, 0], own_sem.at[1, q])
        drain(qbuf.at[q, pl.ds(0, depth - 1)], qsem.at[q])

    def pass_on(q, which):
        pltpu.make_async_remote_copy(
            src_ref=landed(q, which),
            dst_ref=q2buf.at[q - half, which],
            send_sem=osend.at[q - half, which],
            recv_sem=opp_sem.at[q - half, which],
            device_id=((2 - up) * depth + pos, ch),
            device_id_type=MESH,
        ).start()

    def await_p(q, passed):
        drain(landed(q, own, 0, 1), own_sem.at[0, q])
        drain(landed(q, own, 0, depth - 1), psem.at[q])

        @pl.when(outer)
        def _():
            pltpu.make_async_remote_copy(
                src_ref=landed(q, own),
                dst_ref=landed(q, own),
                send_sem=fsend.at[q],
                recv_sem=outer_sem.at[q],
                device_id=((1 + up) * depth + pos, ch),
                device_id_type=MESH,
            ).start()

        if passed:

            @pl.when(center)
            def _():
                pass_on(q, own)

    def await_outer(q, passed):
        @pl.when(center)
        def _():
            drain(landed(q, 1 - own), outer_sem.at[q])
            if passed:
                pass_on(q, 1 - own)

    row = lax.broadcasted_iota(jnp.int32, (128, 128), 0)
    col = lax.broadcasted_iota(jnp.int32, (128, 128), 1)
    eye = (row == col).astype(jnp.bfloat16)
    first = row >= col + up

    def turn(block):
        return lax.dot_general(
            eye, block, (((1,), (1,)), ((), ())), preferred_element_type=jnp.float32
        ).astype(jnp.bfloat16)

    def offset_of(k):
        return off_ref[k - 1] if k else 0

    def rows_from(q, start):
        at = lax.div(start, copies)
        which = lax.rem(start, copies)
        steps = range(layer_rows // 16)
        if copies == 1:
            return jnp.concatenate([pbuf[q, at + step] for step in steps], axis=0)
        return jnp.concatenate([wide[which * groups + at + step] for step in steps], axis=0)

    def window(q, q_layer, offset):
        start = (q_layer - 2 * up) * tiles + (2 * up - 1) * offset + up
        start = lax.min(lax.max(start, -tiles), 2 * tiles + 1) + base
        return jnp.concatenate([rows_from(q, start), rows_from(q, start - 1)], axis=1)

    def folded(grid):
        picked = jnp.where(first, grid[:, :128], grid[:, 128:])
        acc = picked[0:8]
        for b in range(1, 16):
            acc = acc + pltpu.roll(picked[8 * b : 8 * b + 8], 128 - 8 * b, 1)
        return acc

    def dot(left, right):
        return jnp.dot(left, right, preferred_element_type=jnp.float32)

    lo, count = lead - 1, 2 * depth * pieces + 2

    def shifted(q):
        if copies == 1:
            return
        near = pbuf[q, lo : lo + count]
        wide[lo : lo + count] = near
        flat = near.astype(jnp.float32).reshape(count * 16, 128)
        for move in range(1, copies):
            moved = pltpu.roll(flat, count * 16 - move * ch_rows, 0).astype(jnp.bfloat16)
            wide[move * groups + lo : move * groups + lo + count] = moved.reshape(count, 16, 128)

    def own_work(q):
        filt = lax.rem(q + up * half, mine)
        shifted(q)
        turned = turn(qbuf[q].reshape(layer_rows, 128))
        for k in range(blocks):
            sums[k, filt] = folded(dot(turned, window(q, layer, offset_of(k))))

    def far_work(q, which):
        filt = lax.rem(q + up * half, mine)

        @pl.when(center)
        def _():
            drain(q2buf.at[q, which], opp_sem.at[q, which])
            turned = turn(q2buf[q, which].reshape(layer_rows, 128))
            for k in range(blocks):
                grid = dot(turned, window(q, 2 - 2 * up + which, offset_of(k)))
                sums[k, filt] = sums[k, filt] + folded(grid)

    start_p(half)
    start_p(0)
    start_q(half)
    await_p(half, True)
    if half > 1:
        start_p(half + 1)
    await_p(0, False)
    start_q(0)
    await_outer(half, True)

    def pair(kept, carry):
        sent = kept + half
        more = kept + 1 < half
        await_q(sent)

        @pl.when(more)
        def _():
            start_p(kept + 1)

        own_work(sent)

        @pl.when(more)
        def _():
            await_p(sent + 1, True)
            start_q(sent + 1)
            start_q(kept + 1)

        await_outer(kept, False)
        await_q(kept)
        own_work(kept)

        @pl.when(more)
        def _():
            await_p(kept + 1, False)

        far_work(kept, up)

        @pl.when(more)
        def _():
            await_outer(sent + 1, True)

        @pl.when(kept + 2 < half)
        def _():
            start_p(sent + 2)

        far_work(kept, 1 - up)
        return carry

    lax.fori_loop(0, half, pair, 0)

    rolled = sums[...].reshape(blocks * mine * 8, 128)
    small = lax.broadcasted_iota(jnp.int32, rolled.shape, 0)
    for bit in (1, 2, 4):
        rolled = jnp.where((small & bit) != 0, pltpu.roll(rolled, 128 - bit, 1), rolled)
    summed = jnp.sum(rolled.reshape(blocks * mine, 8, 128), axis=1)
    flip = (128 - col) % 128
    order_mat = (row == jnp.where(up == 1, col, flip)).astype(jnp.float32)
    summed = jnp.dot(
        summed, order_mat, precision=lax.Precision.HIGHEST, preferred_element_type=jnp.float32
    )
    for k in range(blocks):
        lags[k] = summed[k * mine : (k + 1) * mine]

    def first_row(at):
        return jnp.minimum((at * piece) // 128, blocks - 2)

    def hand_out(step, carry):
        to = (me + step) % total
        pltpu.make_async_remote_copy(
            src_ref=lags.at[pl.ds(first_row(to // ch_count), 2)],
            dst_ref=parts.at[me],
            send_sem=xsend,
            recv_sem=xrecv,
            device_id=(to // ch_count, to % ch_count),
            device_id_type=MESH,
        ).start()
        return carry

    lax.fori_loop(1, total, hand_out, 0)
    start_row = first_row(ctx)
    parts[me] = lags[pl.ds(start_row, 2)]
    drain(parts.at[pl.ds(0, total - 1)], xrecv)
    for at in range(depth):
        acc = None
        for lay in range(LAYERS):
            for h in range(ch_count):
                term = parts[(lay * depth + at) * ch_count + h]
                acc = term if acc is None else acc + term
        joined[at * mine : (at + 1) * mine, 0:128] = acc[0]
        joined[at * mine : (at + 1) * mine, 128:256] = acc[1]
    skip = ctx * piece - start_row * 128
    out_ref[...] = pltpu.roll(joined[...], lax.rem(256 - skip, 256), 1)[:, :piece]

    drain(parts.at[pl.ds(0, total - 1)], xsend)
    for q in range(mine):
        drain(landed(q, 0, 0, depth - 1), psend.at[q])
        drain(qbuf.at[q, pl.ds(0, depth - 1)], qsend.at[q])

    @pl.when(outer)
    def _():
        for q in range(mine):
            drain(landed(q, 0), fsend.at[q])

    @pl.when(center)
    def _():
        for q in range(half):
            for which in range(2):
                drain(landed(q, 0), osend.at[q, which])


def local(ctx_count, ch_count, saved_input, out_grad, block_offsets, head_len):
    filters, local_ch, tok_dev = saved_input.shape
    tile_count = tok_dev // 128
    rows = tile_count * local_ch
    blocks = block_offsets.shape[0] + 1
    depth = ctx_count // LAYERS
    mine = filters // depth
    half = mine // 2
    copies = 16 // local_ch
    pieces = rows // 16
    groups = 4 * depth * pieces + 4
    piece = blocks * 128 // ctx_count
    total = ctx_count * ch_count
    loss_scale = 1.0 / math.sqrt(tok_dev * ctx_count * local_ch * ch_count)

    def tiled(array):
        split = array.reshape(filters, local_ch, tile_count, 128)
        return jnp.transpose(split, (0, 2, 1, 3)).reshape(filters, pieces, 16, 128)

    bf16, f32 = jnp.bfloat16, jnp.float32
    dma = pltpu.SemaphoreType.DMA
    taps = pl.pallas_call(
        functools.partial(kernel, ctx_count, ch_count, copies),
        out_shape=jax.ShapeDtypeStruct((filters, piece), f32),
        in_specs=[pl.BlockSpec(memory_space=pltpu.SMEM)] + [pl.BlockSpec(memory_space=pl.ANY)] * 2,
        out_specs=pl.BlockSpec(memory_space=pltpu.VMEM),
        scratch_shapes=[
            pltpu.VMEM((mine, groups, 16, 128), bf16),
            pltpu.VMEM((mine, depth, pieces, 16, 128), bf16),
            pltpu.VMEM((half, 2, depth * pieces, 16, 128), bf16),
            pltpu.VMEM((copies * groups, 16, 128), bf16),
            pltpu.VMEM((blocks, mine, 8, 128), f32),
            pltpu.VMEM((blocks, mine, 128), f32),
            pltpu.VMEM((total, 2, mine, 128), f32),
            pltpu.VMEM((filters, 256), f32),
            dma((2, mine)),
            dma((mine,)),
            dma((mine,)),
            dma((mine,)),
            dma((half, 2)),
            dma((mine,)),
            dma((mine,)),
            dma((mine,)),
            dma((half, 2)),
            dma,
            dma,
        ],
        compiler_params=pltpu.CompilerParams(
            collective_id=0, has_side_effects=True, vmem_limit_bytes=60 * 1024 * 1024
        ),
        cost_estimate=pl.CostEstimate(flops=7 * 10**9, bytes_accessed=4 * 10**6, transcendentals=0),
    )(block_offsets, tiled(saved_input), tiled(out_grad))
    lag = lax.broadcasted_iota(jnp.int32, taps.shape, 1) + lax.axis_index("ctx") * piece
    keep = (lag >= 128) | (lag < head_len[0])
    return jnp.where(keep, taps * loss_scale, jnp.zeros_like(taps))


def solution(mesh):
    ctx_count, ch_count = mesh.shape["ctx"], mesh.shape["ch"]
    in_specs = (P(None, "ch", "ctx"), P(None, "ch", "ctx"), P(), P())
    out_specs = P(None, "ctx")
    return jax.shard_map(
        functools.partial(local, ctx_count, ch_count),
        mesh=mesh, in_specs=in_specs, out_specs=out_specs, check_vma=False,
    )
```

```python
import functools
import math

import jax
import jax.numpy as jnp
from jax import lax
from jax.experimental import pallas as pl
from jax.experimental.pallas import tpu as pltpu
from jax.sharding import PartitionSpec as P

LAYERS = 4
MESH = pl.DeviceIdType.MESH


def kernel(
    ctx_count, ch_count, copies,
    off_ref, x_ref, dy_ref, out_ref,
    pbuf, qbuf, q2buf, wide, sums, lags, parts, joined,
    own_sem, psem, qsem, outer_sem, opp_sem, psend, qsend, fsend, osend, bsend, rsend, xsend, xrecv,
):
    filters, pieces = x_ref.shape[:2]
    blocks = lags.shape[0]
    depth = ctx_count // LAYERS
    mine = filters // depth
    half = mine // 2
    cut = half // 2
    layer_rows = depth * pieces * 16
    ch_rows = 16 // copies
    groups = pbuf.shape[1]
    tiles = layer_rows // ch_rows
    base = tiles + copies
    lead = base // copies
    piece = out_ref.shape[1]
    total = ctx_count * ch_count

    ctx = lax.axis_index("ctx")
    ch = lax.axis_index("ch")
    me = ctx * ch_count + ch
    layer, pos = ctx // depth, ctx % depth
    up = layer // 2
    own = layer % 2
    center = own != up
    outer = own == up

    barrier = pltpu.get_barrier_semaphore()

    def greet(step, carry):
        to = lax.rem(me + step, total)
        pl.semaphore_signal(
            barrier, inc=1, device_id=(to // ch_count, to % ch_count), device_id_type=MESH
        )
        return carry

    lax.fori_loop(1, total, greet, 0)

    def landed(q, which, at=0, count=depth):
        return pbuf.at[q, pl.ds(lead + (which * depth + at) * pieces, count * pieces)]

    def drain(ref, sem):
        pltpu.make_async_copy(ref, ref, sem).wait()

    pbuf[:, 0:lead] = jnp.zeros((mine, lead, 16, 128), pbuf.dtype)
    tail = lead + 2 * depth * pieces
    pbuf[:, tail:groups] = jnp.zeros((mine, groups - tail, 16, 128), pbuf.dtype)
    if copies > 1:
        wide[...] = jnp.zeros_like(wide)

    @pl.when(outer)
    def _():
        pbuf[cut:, pl.ds(lead + (1 - own) * depth * pieces, depth * pieces)] = jnp.zeros(
            (mine - cut, depth * pieces, 16, 128), pbuf.dtype
        )

    pl.semaphore_wait(barrier, total - 1)

    def start_layer(src, dst, sem, send_sem, own_idx, q):
        filt = lax.rem(q + up * half, mine)
        pltpu.make_async_copy(src.at[pos * mine + filt], dst, own_sem.at[own_idx, q]).start()
        for step in range(1, depth):
            peer = lax.rem(pos + step, depth)
            pltpu.make_async_remote_copy(
                src_ref=src.at[peer * mine + filt],
                dst_ref=dst,
                send_sem=send_sem.at[q],
                recv_sem=sem.at[q],
                device_id=(layer * depth + peer, ch),
                device_id_type=MESH,
            ).start()

    def start_p(q):
        @pl.when(up == 0)
        def _():
            start_layer(x_ref, landed(q, own, pos, 1), psem, psend, 0, q)

        @pl.when(up == 1)
        def _():
            start_layer(dy_ref, landed(q, own, pos, 1), psem, psend, 0, q)

    def start_q(q):
        @pl.when(up == 0)
        def _():
            start_layer(dy_ref, qbuf.at[q, pos], qsem, qsend, 1, q)

        @pl.when(up == 1)
        def _():
            start_layer(x_ref, qbuf.at[q, pos], qsem, qsend, 1, q)

    def await_q(q):
        drain(qbuf.at[q, 0], own_sem.at[1, q])
        drain(qbuf.at[q, pl.ds(0, depth - 1)], qsem.at[q])

    def pass_on(q, which):
        pltpu.make_async_remote_copy(
            src_ref=landed(q, which),
            dst_ref=q2buf.at[q - half, which],
            send_sem=osend.at[q - half, which],
            recv_sem=opp_sem.at[q - half, which],
            device_id=((2 - up) * depth + pos, ch),
            device_id_type=MESH,
        ).start()

    def await_p(q, passed):
        drain(landed(q, own, 0, 1), own_sem.at[0, q])
        drain(landed(q, own, 0, depth - 1), psem.at[q])

        @pl.when(outer)
        def _():
            pltpu.make_async_remote_copy(
                src_ref=landed(q, own),
                dst_ref=landed(q, own),
                send_sem=fsend.at[q],
                recv_sem=outer_sem.at[q],
                device_id=((1 + up) * depth + pos, ch),
                device_id_type=MESH,
            ).start()

        @pl.when(center & (passed | (q < cut)))
        def _():
            if passed:
                pass_on(q, own)
            else:
                pltpu.make_async_remote_copy(
                    src_ref=landed(q, own),
                    dst_ref=landed(q, own),
                    send_sem=bsend.at[q],
                    recv_sem=outer_sem.at[q],
                    device_id=(3 * up * depth + pos, ch),
                    device_id_type=MESH,
                ).start()

    def await_outer(q, passed):
        @pl.when(center | (q < cut))
        def _():
            drain(landed(q, 1 - own), outer_sem.at[q])
            if passed:
                pass_on(q, 1 - own)

    def relay(q, which):
        @pl.when(center & (q < cut))
        def _():
            drain(q2buf.at[q, which], opp_sem.at[q, which])
            pltpu.make_async_remote_copy(
                src_ref=q2buf.at[q, which],
                dst_ref=q2buf.at[q, which],
                send_sem=rsend.at[q, which],
                recv_sem=opp_sem.at[q, which],
                device_id=(3 * up * depth + pos, ch),
                device_id_type=MESH,
            ).start()

    row = lax.broadcasted_iota(jnp.int32, (128, 128), 0)
    col = lax.broadcasted_iota(jnp.int32, (128, 128), 1)
    eye = (row == col).astype(jnp.bfloat16)
    first = row >= col + up

    def turn(block):
        return lax.dot_general(
            eye, block, (((1,), (1,)), ((), ())), preferred_element_type=jnp.float32
        ).astype(jnp.bfloat16)

    def offset_of(k):
        return off_ref[k - 1] if k else 0

    def rows_from(q, start):
        at = lax.div(start, copies)
        which = lax.rem(start, copies)
        steps = layer_rows // 16
        if copies == 1:
            return pbuf[q, pl.ds(at, steps)].reshape(layer_rows, 128)
        return wide[pl.ds(which * groups + at, steps)].reshape(layer_rows, 128)

    def window(q, q_layer, offset):
        start = (q_layer - 2 * up) * tiles + (2 * up - 1) * offset + up
        start = lax.min(lax.max(start, -tiles), 2 * tiles + 1) + base
        return jnp.concatenate([rows_from(q, start), rows_from(q, start - 1)], axis=1)

    def folded(grid):
        picked = jnp.where(first, grid[:, :128], grid[:, 128:])
        acc = picked[0:8]
        for b in range(1, 16):
            acc = acc + pltpu.roll(picked[8 * b : 8 * b + 8], 128 - 8 * b, 1)
        return acc

    def dot(left, right):
        return jnp.dot(left, right, preferred_element_type=jnp.float32)

    lo, count = lead - 1, 2 * depth * pieces + 2

    def shifted(q):
        if copies == 1:
            return
        near = pbuf[q, lo : lo + count]
        wide[lo : lo + count] = near
        flat = near.astype(jnp.float32).reshape(count * 16, 128)
        for move in range(1, copies):
            moved = pltpu.roll(flat, count * 16 - move * ch_rows, 0).astype(jnp.bfloat16)
            wide[move * groups + lo : move * groups + lo + count] = moved.reshape(count, 16, 128)

    def own_work(q):
        filt = lax.rem(q + up * half, mine)
        shifted(q)
        turned = turn(qbuf[q].reshape(layer_rows, 128))
        for k in range(blocks):
            sums[k, filt] = folded(dot(turned, window(q, layer, offset_of(k))))

    def far_work(q):
        filt = lax.rem(q + up * half, mine)

        @pl.when((center & (q >= cut)) | (outer & (q < cut)))
        def _():
            for which in range(2):
                drain(q2buf.at[q, which], opp_sem.at[q, which])
            left = turn(q2buf[q, 0].reshape(layer_rows, 128))
            right = turn(q2buf[q, 1].reshape(layer_rows, 128))
            far = 2 - 2 * up
            for k in range(blocks):
                grid = dot(left, window(q, far, offset_of(k)))
                grid = grid + dot(right, window(q, far + 1, offset_of(k)))
                sums[k, filt] = sums[k, filt] + folded(grid)

    start_p(half)
    start_p(0)
    start_q(half)
    await_p(half, True)
    if half > 1:
        start_p(half + 1)
    await_p(0, False)
    start_q(0)
    await_outer(half, True)

    def pair(kept, carry):
        sent = kept + half
        more = kept + 1 < half
        await_q(sent)

        @pl.when(more)
        def _():
            start_p(kept + 1)

        own_work(sent)

        @pl.when(more)
        def _():
            await_p(sent + 1, True)
            start_q(sent + 1)
            start_q(kept + 1)

        relay(kept, up)
        await_outer(kept, False)
        await_q(kept)
        own_work(kept)

        @pl.when(more)
        def _():
            await_p(kept + 1, False)

        relay(kept, 1 - up)

        @pl.when(more)
        def _():
            await_outer(sent + 1, True)

        @pl.when(kept + 2 < half)
        def _():
            start_p(sent + 2)

        far_work(kept)
        return carry

    lax.fori_loop(0, half, pair, 0)

    rolled = sums[...].reshape(blocks * mine * 8, 128)
    small = lax.broadcasted_iota(jnp.int32, rolled.shape, 0)
    for bit in (1, 2, 4):
        rolled = jnp.where((small & bit) != 0, pltpu.roll(rolled, 128 - bit, 1), rolled)
    summed = jnp.sum(rolled.reshape(blocks * mine, 8, 128), axis=1)
    flip = (128 - col) % 128
    order_mat = (row == jnp.where(up == 1, col, flip)).astype(jnp.float32)
    summed = jnp.dot(
        summed, order_mat, precision=lax.Precision.HIGHEST, preferred_element_type=jnp.float32
    )
    for k in range(blocks):
        lags[k] = summed[k * mine : (k + 1) * mine]

    def first_row(at):
        return jnp.minimum((at * piece) // 128, blocks - 2)

    def hand_out(step, carry):
        to = (me + step) % total
        pltpu.make_async_remote_copy(
            src_ref=lags.at[pl.ds(first_row(to // ch_count), 2)],
            dst_ref=parts.at[me],
            send_sem=xsend,
            recv_sem=xrecv,
            device_id=(to // ch_count, to % ch_count),
            device_id_type=MESH,
        ).start()
        return carry

    lax.fori_loop(1, total, hand_out, 0)
    start_row = first_row(ctx)
    parts[me] = lags[pl.ds(start_row, 2)]
    drain(parts.at[pl.ds(0, total - 1)], xrecv)
    for at in range(depth):
        acc = None
        for lay in range(LAYERS):
            for h in range(ch_count):
                term = parts[(lay * depth + at) * ch_count + h]
                acc = term if acc is None else acc + term
        joined[at * mine : (at + 1) * mine, 0:128] = acc[0]
        joined[at * mine : (at + 1) * mine, 128:256] = acc[1]
    skip = ctx * piece - start_row * 128
    out_ref[...] = pltpu.roll(joined[...], lax.rem(256 - skip, 256), 1)[:, :piece]

    drain(parts.at[pl.ds(0, total - 1)], xsend)
    for q in range(mine):
        drain(landed(q, 0, 0, depth - 1), psend.at[q])
        drain(qbuf.at[q, pl.ds(0, depth - 1)], qsend.at[q])

    @pl.when(outer)
    def _():
        for q in range(mine):
            drain(landed(q, 0), fsend.at[q])

    @pl.when(center)
    def _():
        for q in range(half):
            for which in range(2):
                drain(landed(q, 0), osend.at[q, which])
        for q in range(cut):
            drain(landed(q, 0), bsend.at[q])
            for which in range(2):
                drain(q2buf.at[q, which], rsend.at[q, which])


def local(ctx_count, ch_count, saved_input, out_grad, block_offsets, head_len):
    filters, local_ch, tok_dev = saved_input.shape
    tile_count = tok_dev // 128
    rows = tile_count * local_ch
    blocks = block_offsets.shape[0] + 1
    depth = ctx_count // LAYERS
    mine = filters // depth
    half = mine // 2
    copies = 16 // local_ch
    pieces = rows // 16
    groups = 4 * depth * pieces + 4
    piece = blocks * 128 // ctx_count
    total = ctx_count * ch_count
    loss_scale = 1.0 / math.sqrt(tok_dev * ctx_count * local_ch * ch_count)

    def tiled(array):
        split = array.reshape(filters, local_ch, tile_count, 128)
        return jnp.transpose(split, (0, 2, 1, 3)).reshape(filters, pieces, 16, 128)

    bf16, f32 = jnp.bfloat16, jnp.float32
    dma = pltpu.SemaphoreType.DMA
    taps = pl.pallas_call(
        functools.partial(kernel, ctx_count, ch_count, copies),
        out_shape=jax.ShapeDtypeStruct((filters, piece), f32),
        in_specs=[pl.BlockSpec(memory_space=pltpu.SMEM)] + [pl.BlockSpec(memory_space=pl.ANY)] * 2,
        out_specs=pl.BlockSpec(memory_space=pltpu.VMEM),
        scratch_shapes=[
            pltpu.VMEM((mine, groups, 16, 128), bf16),
            pltpu.VMEM((mine, depth, pieces, 16, 128), bf16),
            pltpu.VMEM((half, 2, depth * pieces, 16, 128), bf16),
            pltpu.VMEM((copies * groups, 16, 128), bf16),
            pltpu.VMEM((blocks, mine, 8, 128), f32),
            pltpu.VMEM((blocks, mine, 128), f32),
            pltpu.VMEM((total, 2, mine, 128), f32),
            pltpu.VMEM((filters, 256), f32),
            dma((2, mine)),
            dma((mine,)),
            dma((mine,)),
            dma((mine,)),
            dma((half, 2)),
            dma((mine,)),
            dma((mine,)),
            dma((mine,)),
            dma((half, 2)),
            dma((half,)),
            dma((half, 2)),
            dma,
            dma,
        ],
        compiler_params=pltpu.CompilerParams(
            collective_id=0, has_side_effects=True, vmem_limit_bytes=60 * 1024 * 1024
        ),
        cost_estimate=pl.CostEstimate(flops=7 * 10**9, bytes_accessed=4 * 10**6, transcendentals=0),
    )(block_offsets, tiled(saved_input), tiled(out_grad))
    lag = lax.broadcasted_iota(jnp.int32, taps.shape, 1) + lax.axis_index("ctx") * piece
    keep = (lag >= 128) | (lag < head_len[0])
    return jnp.where(keep, taps * loss_scale, jnp.zeros_like(taps))


def solution(mesh):
    ctx_count, ch_count = mesh.shape["ctx"], mesh.shape["ch"]
    in_specs = (P(None, "ch", "ctx"), P(None, "ch", "ctx"), P(), P())
    out_specs = P(None, "ctx")
    return jax.shard_map(
        functools.partial(local, ctx_count, ch_count),
        mesh=mesh, in_specs=in_specs, out_specs=out_specs, check_vma=False,
    )
```

```python
import functools
import math

import jax
import jax.numpy as jnp
from jax import lax
from jax.experimental import pallas as pl
from jax.experimental.pallas import tpu as pltpu
from jax.sharding import PartitionSpec as P

LAYERS = 4
MESH = pl.DeviceIdType.MESH


def kernel(
    ctx_count, ch_count, copies,
    off_ref, x_ref, dy_ref, out_ref,
    pbuf, qbuf, q2buf, wide, sums, lags, parts, joined,
    own_sem, psem, qsem, outer_sem, opp_sem, psend, qsend, fsend, osend, xsend, xrecv,
):
    filters, pieces = x_ref.shape[:2]
    blocks = lags.shape[0]
    depth = ctx_count // LAYERS
    mine = filters // depth
    half = mine // 2
    layer_rows = depth * pieces * 16
    ch_rows = 16 // copies
    groups = pbuf.shape[1]
    tiles = layer_rows // ch_rows
    base = tiles + copies
    lead = base // copies
    piece = out_ref.shape[1]
    total = ctx_count * ch_count

    ctx = lax.axis_index("ctx")
    ch = lax.axis_index("ch")
    me = ctx * ch_count + ch
    layer, pos = ctx // depth, ctx % depth
    up = layer // 2
    own = layer % 2
    center = own != up
    outer = own == up

    barrier = pltpu.get_barrier_semaphore()

    def greet(step, carry):
        to = lax.rem(me + step, total)
        pl.semaphore_signal(
            barrier, inc=1, device_id=(to // ch_count, to % ch_count), device_id_type=MESH
        )
        return carry

    lax.fori_loop(1, total, greet, 0)

    def landed(q, which, at=0, count=depth):
        return pbuf.at[q, pl.ds(lead + (which * depth + at) * pieces, count * pieces)]

    def drain(ref, sem):
        pltpu.make_async_copy(ref, ref, sem).wait()

    pbuf[:, 0:lead] = jnp.zeros((mine, lead, 16, 128), pbuf.dtype)
    tail = lead + 2 * depth * pieces
    pbuf[:, tail:groups] = jnp.zeros((mine, groups - tail, 16, 128), pbuf.dtype)
    if copies > 1:
        wide[...] = jnp.zeros_like(wide)

    @pl.when(outer)
    def _():
        pbuf[:, pl.ds(lead + (1 - own) * depth * pieces, depth * pieces)] = jnp.zeros(
            (mine, depth * pieces, 16, 128), pbuf.dtype
        )

    pl.semaphore_wait(barrier, total - 1)

    def start_layer(src, dst, sem, send_sem, own_idx, q):
        filt = lax.rem(q + up * half, mine)
        pltpu.make_async_copy(src.at[pos * mine + filt], dst, own_sem.at[own_idx, q]).start()
        for step in range(1, depth):
            peer = lax.rem(pos + step, depth)
            pltpu.make_async_remote_copy(
                src_ref=src.at[peer * mine + filt],
                dst_ref=dst,
                send_sem=send_sem.at[q],
                recv_sem=sem.at[q],
                device_id=(layer * depth + peer, ch),
                device_id_type=MESH,
            ).start()

    def start_p(q):
        @pl.when(up == 0)
        def _():
            start_layer(x_ref, landed(q, own, pos, 1), psem, psend, 0, q)

        @pl.when(up == 1)
        def _():
            start_layer(dy_ref, landed(q, own, pos, 1), psem, psend, 0, q)

    def start_q(q):
        @pl.when(up == 0)
        def _():
            start_layer(dy_ref, qbuf.at[q, pos], qsem, qsend, 1, q)

        @pl.when(up == 1)
        def _():
            start_layer(x_ref, qbuf.at[q, pos], qsem, qsend, 1, q)

    def await_q(q):
        drain(qbuf.at[q, 0], own_sem.at[1, q])
        drain(qbuf.at[q, pl.ds(0, depth - 1)], qsem.at[q])

    def pass_on(q, which):
        pltpu.make_async_remote_copy(
            src_ref=landed(q, which),
            dst_ref=q2buf.at[q - half, which],
            send_sem=osend.at[q - half, which],
            recv_sem=opp_sem.at[q - half, which],
            device_id=((2 - up) * depth + pos, ch),
            device_id_type=MESH,
        ).start()

    def await_p(q, passed):
        drain(landed(q, own, 0, 1), own_sem.at[0, q])
        drain(landed(q, own, 0, depth - 1), psem.at[q])

        @pl.when(outer)
        def _():
            pltpu.make_async_remote_copy(
                src_ref=landed(q, own),
                dst_ref=landed(q, own),
                send_sem=fsend.at[q],
                recv_sem=outer_sem.at[q],
                device_id=((1 + up) * depth + pos, ch),
                device_id_type=MESH,
            ).start()

        if passed:

            @pl.when(center)
            def _():
                pass_on(q, own)

    def await_outer(q, passed):
        @pl.when(center)
        def _():
            drain(landed(q, 1 - own), outer_sem.at[q])
            if passed:
                pass_on(q, 1 - own)

    row = lax.broadcasted_iota(jnp.int32, (128, 128), 0)
    col = lax.broadcasted_iota(jnp.int32, (128, 128), 1)
    eye = (row == col).astype(jnp.bfloat16)
    first = row >= col + up

    def turn(block):
        return lax.dot_general(
            eye, block, (((1,), (1,)), ((), ())), preferred_element_type=jnp.float32
        ).astype(jnp.bfloat16)

    def offset_of(k):
        return off_ref[k - 1] if k else 0

    def rows_from(q, start):
        at = lax.div(start, copies)
        which = lax.rem(start, copies)
        steps = layer_rows // 16
        if copies == 1:
            return pbuf[q, pl.ds(at, steps)].reshape(layer_rows, 128)
        return wide[pl.ds(which * groups + at, steps)].reshape(layer_rows, 128)

    def window(q, q_layer, offset):
        start = (q_layer - 2 * up) * tiles + (2 * up - 1) * offset + up
        start = lax.min(lax.max(start, -tiles), 2 * tiles + 1) + base
        return jnp.concatenate([rows_from(q, start), rows_from(q, start - 1)], axis=1)

    def folded(grid):
        picked = jnp.where(first, grid[:, :128], grid[:, 128:])
        acc = picked[0:8]
        for b in range(1, 16):
            acc = acc + pltpu.roll(picked[8 * b : 8 * b + 8], 128 - 8 * b, 1)
        return acc

    def dot(left, right):
        return jnp.dot(left, right, preferred_element_type=jnp.float32)

    lo, count = lead - 1, 2 * depth * pieces + 2

    def shifted(q):
        if copies == 1:
            return
        near = pbuf[q, lo : lo + count]
        wide[lo : lo + count] = near
        flat = near.astype(jnp.float32).reshape(count * 16, 128)
        for move in range(1, copies):
            moved = pltpu.roll(flat, count * 16 - move * ch_rows, 0).astype(jnp.bfloat16)
            wide[move * groups + lo : move * groups + lo + count] = moved.reshape(count, 16, 128)

    def own_work(q):
        filt = lax.rem(q + up * half, mine)
        shifted(q)
        turned = turn(qbuf[q].reshape(layer_rows, 128))
        for k in range(blocks):
            sums[k, filt] = folded(dot(turned, window(q, layer, offset_of(k))))

    def far_work(q):
        filt = lax.rem(q + up * half, mine)

        @pl.when(center)
        def _():
            for which in range(2):
                drain(q2buf.at[q, which], opp_sem.at[q, which])
            left = turn(q2buf[q, 0].reshape(layer_rows, 128))
            right = turn(q2buf[q, 1].reshape(layer_rows, 128))
            far = 2 - 2 * up
            for k in range(blocks):
                grid = dot(left, window(q, far, offset_of(k)))
                grid = grid + dot(right, window(q, far + 1, offset_of(k)))
                sums[k, filt] = sums[k, filt] + folded(grid)

    order = [q for kept in range(half) for q in (kept + half, kept)]
    start_p(order[0])
    for before, after in zip(order, order[1:]):
        start_p(after)
        start_q(before)
    start_q(order[-1])
    await_p(half, True)
    await_p(0, False)
    await_outer(half, True)

    def pair(kept, carry):
        sent = kept + half
        more = kept + 1 < half
        await_q(sent)
        own_work(sent)

        @pl.when(more)
        def _():
            await_p(sent + 1, True)

        await_outer(kept, False)
        await_q(kept)
        own_work(kept)

        @pl.when(more)
        def _():
            await_p(kept + 1, False)
            await_outer(sent + 1, True)

        far_work(kept)
        return carry

    lax.fori_loop(0, half, pair, 0)

    rolled = sums[...].reshape(blocks * mine * 8, 128)
    small = lax.broadcasted_iota(jnp.int32, rolled.shape, 0)
    for bit in (1, 2, 4):
        rolled = jnp.where((small & bit) != 0, pltpu.roll(rolled, 128 - bit, 1), rolled)
    summed = jnp.sum(rolled.reshape(blocks * mine, 8, 128), axis=1)
    flip = (128 - col) % 128
    order_mat = (row == jnp.where(up == 1, col, flip)).astype(jnp.float32)
    summed = jnp.dot(
        summed, order_mat, precision=lax.Precision.HIGHEST, preferred_element_type=jnp.float32
    )
    for k in range(blocks):
        lags[k] = summed[k * mine : (k + 1) * mine]

    def first_row(at):
        return jnp.minimum((at * piece) // 128, blocks - 2)

    def hand_out(step, carry):
        to = (me + step) % total
        pltpu.make_async_remote_copy(
            src_ref=lags.at[pl.ds(first_row(to // ch_count), 2)],
            dst_ref=parts.at[me],
            send_sem=xsend,
            recv_sem=xrecv,
            device_id=(to // ch_count, to % ch_count),
            device_id_type=MESH,
        ).start()
        return carry

    lax.fori_loop(1, total, hand_out, 0)
    start_row = first_row(ctx)
    parts[me] = lags[pl.ds(start_row, 2)]
    drain(parts.at[pl.ds(0, total - 1)], xrecv)
    for at in range(depth):
        acc = None
        for lay in range(LAYERS):
            for h in range(ch_count):
                term = parts[(lay * depth + at) * ch_count + h]
                acc = term if acc is None else acc + term
        joined[at * mine : (at + 1) * mine, 0:128] = acc[0]
        joined[at * mine : (at + 1) * mine, 128:256] = acc[1]
    skip = ctx * piece - start_row * 128
    out_ref[...] = pltpu.roll(joined[...], lax.rem(256 - skip, 256), 1)[:, :piece]

    drain(parts.at[pl.ds(0, total - 1)], xsend)
    for q in range(mine):
        drain(landed(q, 0, 0, depth - 1), psend.at[q])
        drain(qbuf.at[q, pl.ds(0, depth - 1)], qsend.at[q])

    @pl.when(outer)
    def _():
        for q in range(mine):
            drain(landed(q, 0), fsend.at[q])

    @pl.when(center)
    def _():
        for q in range(half):
            for which in range(2):
                drain(landed(q, 0), osend.at[q, which])


def local(ctx_count, ch_count, saved_input, out_grad, block_offsets, head_len):
    filters, local_ch, tok_dev = saved_input.shape
    tile_count = tok_dev // 128
    rows = tile_count * local_ch
    blocks = block_offsets.shape[0] + 1
    depth = ctx_count // LAYERS
    mine = filters // depth
    half = mine // 2
    copies = 16 // local_ch
    pieces = rows // 16
    groups = 4 * depth * pieces + 4
    piece = blocks * 128 // ctx_count
    total = ctx_count * ch_count
    loss_scale = 1.0 / math.sqrt(tok_dev * ctx_count * local_ch * ch_count)

    def tiled(array):
        split = array.reshape(filters, local_ch, tile_count, 128)
        return jnp.transpose(split, (0, 2, 1, 3)).reshape(filters, pieces, 16, 128)

    bf16, f32 = jnp.bfloat16, jnp.float32
    dma = pltpu.SemaphoreType.DMA
    taps = pl.pallas_call(
        functools.partial(kernel, ctx_count, ch_count, copies),
        out_shape=jax.ShapeDtypeStruct((filters, piece), f32),
        in_specs=[pl.BlockSpec(memory_space=pltpu.SMEM)] + [pl.BlockSpec(memory_space=pl.ANY)] * 2,
        out_specs=pl.BlockSpec(memory_space=pltpu.VMEM),
        scratch_shapes=[
            pltpu.VMEM((mine, groups, 16, 128), bf16),
            pltpu.VMEM((mine, depth, pieces, 16, 128), bf16),
            pltpu.VMEM((half, 2, depth * pieces, 16, 128), bf16),
            pltpu.VMEM((copies * groups, 16, 128), bf16),
            pltpu.VMEM((blocks, mine, 8, 128), f32),
            pltpu.VMEM((blocks, mine, 128), f32),
            pltpu.VMEM((total, 2, mine, 128), f32),
            pltpu.VMEM((filters, 256), f32),
            dma((2, mine)),
            dma((mine,)),
            dma((mine,)),
            dma((mine,)),
            dma((half, 2)),
            dma((mine,)),
            dma((mine,)),
            dma((mine,)),
            dma((half, 2)),
            dma,
            dma,
        ],
        compiler_params=pltpu.CompilerParams(
            collective_id=0, has_side_effects=True, vmem_limit_bytes=60 * 1024 * 1024
        ),
        cost_estimate=pl.CostEstimate(flops=7 * 10**9, bytes_accessed=4 * 10**6, transcendentals=0),
    )(block_offsets, tiled(saved_input), tiled(out_grad))
    lag = lax.broadcasted_iota(jnp.int32, taps.shape, 1) + lax.axis_index("ctx") * piece
    keep = (lag >= 128) | (lag < head_len[0])
    return jnp.where(keep, taps * loss_scale, jnp.zeros_like(taps))


def solution(mesh):
    ctx_count, ch_count = mesh.shape["ctx"], mesh.shape["ch"]
    in_specs = (P(None, "ch", "ctx"), P(None, "ch", "ctx"), P(), P())
    out_specs = P(None, "ctx")
    return jax.shard_map(
        functools.partial(local, ctx_count, ch_count),
        mesh=mesh, in_specs=in_specs, out_specs=out_specs, check_vma=False,
    )
```

```python
import functools
import math

import jax
import jax.numpy as jnp
from jax import lax
from jax.experimental import pallas as pl
from jax.experimental.pallas import tpu as pltpu
from jax.sharding import PartitionSpec as P

LAYERS = 4
MESH = pl.DeviceIdType.MESH


def kernel(
    ctx_count, ch_count, copies,
    off_ref, x_ref, dy_ref, out_ref,
    pbuf, qbuf, q2buf, wide, sums, lags, parts, joined,
    own_sem, psem, qsem, outer_sem, opp_sem, psend, qsend, fsend, osend, xsend, xrecv,
):
    filters, pieces = x_ref.shape[:2]
    blocks = lags.shape[0]
    depth = ctx_count // LAYERS
    mine = filters // depth
    half = mine // 2
    layer_rows = depth * pieces * 16
    ch_rows = 16 // copies
    groups = pbuf.shape[1]
    tiles = layer_rows // ch_rows
    base = tiles + copies
    lead = base // copies
    piece = out_ref.shape[1]
    total = ctx_count * ch_count

    ctx = lax.axis_index("ctx")
    ch = lax.axis_index("ch")
    me = ctx * ch_count + ch
    layer, pos = ctx // depth, ctx % depth
    up = layer // 2
    own = layer % 2
    center = own != up
    outer = own == up

    barrier = pltpu.get_barrier_semaphore()

    def greet(step, carry):
        to = lax.rem(me + step, total)
        pl.semaphore_signal(
            barrier, inc=1, device_id=(to // ch_count, to % ch_count), device_id_type=MESH
        )
        return carry

    lax.fori_loop(1, total, greet, 0)

    def landed(q, which, at=0, count=depth):
        return pbuf.at[q, pl.ds(lead + (which * depth + at) * pieces, count * pieces)]

    def drain(ref, sem):
        pltpu.make_async_copy(ref, ref, sem).wait()

    pbuf[:, 0:lead] = jnp.zeros((mine, lead, 16, 128), pbuf.dtype)
    tail = lead + 2 * depth * pieces
    pbuf[:, tail:groups] = jnp.zeros((mine, groups - tail, 16, 128), pbuf.dtype)
    if copies > 1:
        wide[...] = jnp.zeros_like(wide)

    @pl.when(outer)
    def _():
        pbuf[:, pl.ds(lead + (1 - own) * depth * pieces, depth * pieces)] = jnp.zeros(
            (mine, depth * pieces, 16, 128), pbuf.dtype
        )

    pl.semaphore_wait(barrier, total - 1)

    def start_layer(src, dst, sem, send_sem, own_idx, q):
        filt = lax.rem(q + up * half, mine)
        pltpu.make_async_copy(src.at[pos * mine + filt], dst, own_sem.at[own_idx, q]).start()
        for step in range(1, depth):
            peer = lax.rem(pos + step, depth)
            pltpu.make_async_remote_copy(
                src_ref=src.at[peer * mine + filt],
                dst_ref=dst,
                send_sem=send_sem.at[q],
                recv_sem=sem.at[q],
                device_id=(layer * depth + peer, ch),
                device_id_type=MESH,
            ).start()

    def start_p(q):
        @pl.when(up == 0)
        def _():
            start_layer(x_ref, landed(q, own, pos, 1), psem, psend, 0, q)

        @pl.when(up == 1)
        def _():
            start_layer(dy_ref, landed(q, own, pos, 1), psem, psend, 0, q)

    def start_q(q):
        @pl.when(up == 0)
        def _():
            start_layer(dy_ref, qbuf.at[q, pos], qsem, qsend, 1, q)

        @pl.when(up == 1)
        def _():
            start_layer(x_ref, qbuf.at[q, pos], qsem, qsend, 1, q)

    def await_q(q):
        drain(qbuf.at[q, 0], own_sem.at[1, q])
        drain(qbuf.at[q, pl.ds(0, depth - 1)], qsem.at[q])

    def pass_on(q, which):
        pltpu.make_async_remote_copy(
            src_ref=landed(q, which),
            dst_ref=q2buf.at[q - half, which],
            send_sem=osend.at[q - half, which],
            recv_sem=opp_sem.at[q - half, which],
            device_id=((2 - up) * depth + pos, ch),
            device_id_type=MESH,
        ).start()

    def await_p(q, passed):
        drain(landed(q, own, 0, 1), own_sem.at[0, q])
        drain(landed(q, own, 0, depth - 1), psem.at[q])

        @pl.when(outer)
        def _():
            pltpu.make_async_remote_copy(
                src_ref=landed(q, own),
                dst_ref=landed(q, own),
                send_sem=fsend.at[q],
                recv_sem=outer_sem.at[q],
                device_id=((1 + up) * depth + pos, ch),
                device_id_type=MESH,
            ).start()

        if passed:

            @pl.when(center)
            def _():
                pass_on(q, own)

    def await_outer(q, passed):
        @pl.when(center)
        def _():
            drain(landed(q, 1 - own), outer_sem.at[q])
            if passed:
                pass_on(q, 1 - own)

    row = lax.broadcasted_iota(jnp.int32, (128, 128), 0)
    col = lax.broadcasted_iota(jnp.int32, (128, 128), 1)
    eye = (row == col).astype(jnp.bfloat16)
    first = row >= col + up

    def turn(block):
        return lax.dot_general(
            eye, block, (((1,), (1,)), ((), ())), preferred_element_type=jnp.float32
        ).astype(jnp.bfloat16)

    def offset_of(k):
        return off_ref[k - 1] if k else 0

    def rows_from(q, start):
        at = lax.div(start, copies)
        which = lax.rem(start, copies)
        steps = layer_rows // 16
        if copies == 1:
            return pbuf[q, pl.ds(at, steps)].reshape(layer_rows, 128)
        return wide[pl.ds(which * groups + at, steps)].reshape(layer_rows, 128)

    def window(q, q_layer, offset):
        start = (q_layer - 2 * up) * tiles + (2 * up - 1) * offset + up
        start = lax.min(lax.max(start, -tiles), 2 * tiles + 1) + base
        return jnp.concatenate([rows_from(q, start), rows_from(q, start - 1)], axis=1)

    def folded(grid):
        picked = jnp.where(first, grid[:, :128], grid[:, 128:])
        acc = picked[0:8]
        for b in range(1, 16):
            acc = acc + pltpu.roll(picked[8 * b : 8 * b + 8], 128 - 8 * b, 1)
        return acc

    def dot(left, right):
        return jnp.dot(left, right, preferred_element_type=jnp.float32)

    lo, count = lead - 1, 2 * depth * pieces + 2

    def shifted(q):
        if copies == 1:
            return
        near = pbuf[q, lo : lo + count]
        wide[lo : lo + count] = near
        flat = near.astype(jnp.float32).reshape(count * 16, 128)
        for move in range(1, copies):
            moved = pltpu.roll(flat, count * 16 - move * ch_rows, 0).astype(jnp.bfloat16)
            wide[move * groups + lo : move * groups + lo + count] = moved.reshape(count, 16, 128)

    def own_work(q):
        filt = lax.rem(q + up * half, mine)
        shifted(q)
        turned = turn(qbuf[q].reshape(layer_rows, 128))
        for k in range(blocks):
            sums[k, filt] = folded(dot(turned, window(q, layer, offset_of(k))))

    def far_work(q):
        filt = lax.rem(q + up * half, mine)

        @pl.when(center)
        def _():
            for which in range(2):
                drain(q2buf.at[q, which], opp_sem.at[q, which])
            left = turn(q2buf[q, 0].reshape(layer_rows, 128))
            right = turn(q2buf[q, 1].reshape(layer_rows, 128))
            far = 2 - 2 * up
            for k in range(blocks):
                grid = dot(left, window(q, far, offset_of(k)))
                grid = grid + dot(right, window(q, far + 1, offset_of(k)))
                sums[k, filt] = sums[k, filt] + folded(grid)

    order = list(range(half, mine)) + list(range(half))
    for q in order:
        start_p(q)
    for q in order:
        start_q(q)
    for q in range(half, mine):
        await_p(q, True)
    for q in range(half, mine):
        await_outer(q, True)
    for q in range(half):
        await_p(q, False)

    def sent_work(index, carry):
        await_q(half + index)
        own_work(half + index)
        return carry

    def kept_work(q, carry):
        await_outer(q, False)
        await_q(q)
        own_work(q)
        far_work(q)
        return carry

    lax.fori_loop(0, mine - half, sent_work, 0)
    lax.fori_loop(0, half, kept_work, 0)

    rolled = sums[...].reshape(blocks * mine * 8, 128)
    small = lax.broadcasted_iota(jnp.int32, rolled.shape, 0)
    for bit in (1, 2, 4):
        rolled = jnp.where((small & bit) != 0, pltpu.roll(rolled, 128 - bit, 1), rolled)
    summed = jnp.sum(rolled.reshape(blocks * mine, 8, 128), axis=1)
    flip = (128 - col) % 128
    order_mat = (row == jnp.where(up == 1, col, flip)).astype(jnp.float32)
    summed = jnp.dot(
        summed, order_mat, precision=lax.Precision.HIGHEST, preferred_element_type=jnp.float32
    )
    for k in range(blocks):
        lags[k] = summed[k * mine : (k + 1) * mine]

    def first_row(at):
        return jnp.minimum((at * piece) // 128, blocks - 2)

    def hand_out(step, carry):
        to = (me + step) % total
        pltpu.make_async_remote_copy(
            src_ref=lags.at[pl.ds(first_row(to // ch_count), 2)],
            dst_ref=parts.at[me],
            send_sem=xsend,
            recv_sem=xrecv,
            device_id=(to // ch_count, to % ch_count),
            device_id_type=MESH,
        ).start()
        return carry

    lax.fori_loop(1, total, hand_out, 0)
    start_row = first_row(ctx)
    parts[me] = lags[pl.ds(start_row, 2)]
    drain(parts.at[pl.ds(0, total - 1)], xrecv)
    for at in range(depth):
        acc = None
        for lay in range(LAYERS):
            for h in range(ch_count):
                term = parts[(lay * depth + at) * ch_count + h]
                acc = term if acc is None else acc + term
        joined[at * mine : (at + 1) * mine, 0:128] = acc[0]
        joined[at * mine : (at + 1) * mine, 128:256] = acc[1]
    skip = ctx * piece - start_row * 128
    out_ref[...] = pltpu.roll(joined[...], lax.rem(256 - skip, 256), 1)[:, :piece]

    drain(parts.at[pl.ds(0, total - 1)], xsend)
    for q in range(mine):
        drain(landed(q, 0, 0, depth - 1), psend.at[q])
        drain(qbuf.at[q, pl.ds(0, depth - 1)], qsend.at[q])

    @pl.when(outer)
    def _():
        for q in range(mine):
            drain(landed(q, 0), fsend.at[q])

    @pl.when(center)
    def _():
        for q in range(half):
            for which in range(2):
                drain(landed(q, 0), osend.at[q, which])


def local(ctx_count, ch_count, saved_input, out_grad, block_offsets, head_len):
    filters, local_ch, tok_dev = saved_input.shape
    tile_count = tok_dev // 128
    rows = tile_count * local_ch
    blocks = block_offsets.shape[0] + 1
    depth = ctx_count // LAYERS
    mine = filters // depth
    half = mine // 2
    copies = 16 // local_ch
    pieces = rows // 16
    groups = 4 * depth * pieces + 4
    piece = blocks * 128 // ctx_count
    total = ctx_count * ch_count
    loss_scale = 1.0 / math.sqrt(tok_dev * ctx_count * local_ch * ch_count)

    def tiled(array):
        split = array.reshape(filters, local_ch, tile_count, 128)
        return jnp.transpose(split, (0, 2, 1, 3)).reshape(filters, pieces, 16, 128)

    bf16, f32 = jnp.bfloat16, jnp.float32
    dma = pltpu.SemaphoreType.DMA
    taps = pl.pallas_call(
        functools.partial(kernel, ctx_count, ch_count, copies),
        out_shape=jax.ShapeDtypeStruct((filters, piece), f32),
        in_specs=[pl.BlockSpec(memory_space=pltpu.SMEM)] + [pl.BlockSpec(memory_space=pl.ANY)] * 2,
        out_specs=pl.BlockSpec(memory_space=pltpu.VMEM),
        scratch_shapes=[
            pltpu.VMEM((mine, groups, 16, 128), bf16),
            pltpu.VMEM((mine, depth, pieces, 16, 128), bf16),
            pltpu.VMEM((half, 2, depth * pieces, 16, 128), bf16),
            pltpu.VMEM((copies * groups, 16, 128), bf16),
            pltpu.VMEM((blocks, mine, 8, 128), f32),
            pltpu.VMEM((blocks, mine, 128), f32),
            pltpu.VMEM((total, 2, mine, 128), f32),
            pltpu.VMEM((filters, 256), f32),
            dma((2, mine)),
            dma((mine,)),
            dma((mine,)),
            dma((mine,)),
            dma((half, 2)),
            dma((mine,)),
            dma((mine,)),
            dma((mine,)),
            dma((half, 2)),
            dma,
            dma,
        ],
        compiler_params=pltpu.CompilerParams(
            collective_id=0, has_side_effects=True, vmem_limit_bytes=60 * 1024 * 1024
        ),
        cost_estimate=pl.CostEstimate(flops=7 * 10**9, bytes_accessed=4 * 10**6, transcendentals=0),
    )(block_offsets, tiled(saved_input), tiled(out_grad))
    lag = lax.broadcasted_iota(jnp.int32, taps.shape, 1) + lax.axis_index("ctx") * piece
    keep = (lag >= 128) | (lag < head_len[0])
    return jnp.where(keep, taps * loss_scale, jnp.zeros_like(taps))


def solution(mesh):
    ctx_count, ch_count = mesh.shape["ctx"], mesh.shape["ch"]
    in_specs = (P(None, "ch", "ctx"), P(None, "ch", "ctx"), P(), P())
    out_specs = P(None, "ctx")
    return jax.shard_map(
        functools.partial(local, ctx_count, ch_count),
        mesh=mesh, in_specs=in_specs, out_specs=out_specs, check_vma=False,
    )
```

```python
import functools
import math

import jax
import jax.numpy as jnp
from jax import lax
from jax.experimental import pallas as pl
from jax.experimental.pallas import tpu as pltpu
from jax.sharding import PartitionSpec as P

LAYERS = 4
MESH = pl.DeviceIdType.MESH


def kernel(
    ctx_count, ch_count, copies,
    off_ref, x_ref, dy_ref, out_ref,
    pbuf, qbuf, q2buf, wide, sums, lags, parts, joined,
    own_sem, psem, qsem, outer_sem, opp_sem, psend, qsend, fsend, osend, xsend, xrecv,
):
    filters, pieces = x_ref.shape[:2]
    blocks = lags.shape[0]
    depth = ctx_count // LAYERS
    mine = filters // depth
    half = mine // 2
    layer_rows = depth * pieces * 16
    ch_rows = 16 // copies
    groups = pbuf.shape[1]
    tiles = layer_rows // ch_rows
    base = tiles + copies
    lead = base // copies
    piece = out_ref.shape[1]
    total = ctx_count * ch_count

    ctx = lax.axis_index("ctx")
    ch = lax.axis_index("ch")
    me = ctx * ch_count + ch
    layer, pos = ctx // depth, ctx % depth
    up = layer // 2
    own = layer % 2
    center = own != up
    outer = own == up

    barrier = pltpu.get_barrier_semaphore()

    def greet(step, carry):
        to = lax.rem(me + step, total)
        pl.semaphore_signal(
            barrier, inc=1, device_id=(to // ch_count, to % ch_count), device_id_type=MESH
        )
        return carry

    lax.fori_loop(1, total, greet, 0)

    def landed(q, which, at=0, count=depth):
        return pbuf.at[q, pl.ds(lead + (which * depth + at) * pieces, count * pieces)]

    def drain(ref, sem):
        pltpu.make_async_copy(ref, ref, sem).wait()

    pbuf[:, 0:lead] = jnp.zeros((mine, lead, 16, 128), pbuf.dtype)
    tail = lead + 2 * depth * pieces
    pbuf[:, tail:groups] = jnp.zeros((mine, groups - tail, 16, 128), pbuf.dtype)
    if copies > 1:
        wide[...] = jnp.zeros_like(wide)

    @pl.when(outer)
    def _():
        pbuf[:, pl.ds(lead + (1 - own) * depth * pieces, depth * pieces)] = jnp.zeros(
            (mine, depth * pieces, 16, 128), pbuf.dtype
        )

    pl.semaphore_wait(barrier, total - 1)

    def start_layer(src, dst, sem, send_sem, own_idx, q):
        filt = lax.rem(q + up * half, mine)
        pltpu.make_async_copy(src.at[pos * mine + filt], dst, own_sem.at[own_idx, q]).start()
        for step in range(1, depth):
            peer = lax.rem(pos + step, depth)
            pltpu.make_async_remote_copy(
                src_ref=src.at[peer * mine + filt],
                dst_ref=dst,
                send_sem=send_sem.at[q],
                recv_sem=sem.at[q],
                device_id=(layer * depth + peer, ch),
                device_id_type=MESH,
            ).start()

    def start_p(q):
        @pl.when(up == 0)
        def _():
            start_layer(x_ref, landed(q, own, pos, 1), psem, psend, 0, q)

        @pl.when(up == 1)
        def _():
            start_layer(dy_ref, landed(q, own, pos, 1), psem, psend, 0, q)

    def start_q(q):
        @pl.when(up == 0)
        def _():
            start_layer(dy_ref, qbuf.at[q, pos], qsem, qsend, 1, q)

        @pl.when(up == 1)
        def _():
            start_layer(x_ref, qbuf.at[q, pos], qsem, qsend, 1, q)

    def await_q(q):
        drain(qbuf.at[q, 0], own_sem.at[1, q])
        drain(qbuf.at[q, pl.ds(0, depth - 1)], qsem.at[q])

    def pass_on(q, which):
        pltpu.make_async_remote_copy(
            src_ref=landed(q, which),
            dst_ref=q2buf.at[q - half, which],
            send_sem=osend.at[q - half, which],
            recv_sem=opp_sem.at[q - half, which],
            device_id=((2 - up) * depth + pos, ch),
            device_id_type=MESH,
        ).start()

    def await_p(q, passed):
        drain(landed(q, own, 0, 1), own_sem.at[0, q])
        drain(landed(q, own, 0, depth - 1), psem.at[q])

        @pl.when(outer)
        def _():
            pltpu.make_async_remote_copy(
                src_ref=landed(q, own),
                dst_ref=landed(q, own),
                send_sem=fsend.at[q],
                recv_sem=outer_sem.at[q],
                device_id=((1 + up) * depth + pos, ch),
                device_id_type=MESH,
            ).start()

        if passed:

            @pl.when(center)
            def _():
                pass_on(q, own)

    def await_outer(q, passed):
        @pl.when(center)
        def _():
            drain(landed(q, 1 - own), outer_sem.at[q])
            if passed:
                pass_on(q, 1 - own)

    row = lax.broadcasted_iota(jnp.int32, (128, 128), 0)
    col = lax.broadcasted_iota(jnp.int32, (128, 128), 1)
    eye = (row == col).astype(jnp.bfloat16)
    first = row >= col + up

    def turn(block):
        return lax.dot_general(
            eye, block, (((1,), (1,)), ((), ())), preferred_element_type=jnp.float32
        ).astype(jnp.bfloat16)

    def offset_of(k):
        return off_ref[k - 1] if k else 0

    def rows_from(q, start):
        at = lax.div(start, copies)
        which = lax.rem(start, copies)
        steps = layer_rows // 16
        if copies == 1:
            return pbuf[q, pl.ds(at, steps)].reshape(layer_rows, 128)
        return wide[pl.ds(which * groups + at, steps)].reshape(layer_rows, 128)

    def window(q, q_layer, offset):
        start = (q_layer - 2 * up) * tiles + (2 * up - 1) * offset + up
        start = lax.min(lax.max(start, -tiles), 2 * tiles + 1) + base
        return jnp.concatenate([rows_from(q, start), rows_from(q, start - 1)], axis=1)

    def folded(grid):
        picked = jnp.where(first, grid[:, :128], grid[:, 128:])
        acc = picked[0:8]
        for b in range(1, 16):
            acc = acc + pltpu.roll(picked[8 * b : 8 * b + 8], 128 - 8 * b, 1)
        return acc

    def dot(left, right):
        return jnp.dot(left, right, preferred_element_type=jnp.float32)

    lo, count = lead - 1, 2 * depth * pieces + 2

    def shifted(q):
        if copies == 1:
            return
        near = pbuf[q, lo : lo + count]
        wide[lo : lo + count] = near
        flat = near.astype(jnp.float32).reshape(count * 16, 128)
        for move in range(1, copies):
            moved = pltpu.roll(flat, count * 16 - move * ch_rows, 0).astype(jnp.bfloat16)
            wide[move * groups + lo : move * groups + lo + count] = moved.reshape(count, 16, 128)

    def own_work(q):
        filt = lax.rem(q + up * half, mine)
        shifted(q)
        turned = turn(qbuf[q].reshape(layer_rows, 128))
        for k in range(blocks):
            sums[k, filt] = folded(dot(turned, window(q, layer, offset_of(k))))

    def far_work(q):
        filt = lax.rem(q + up * half, mine)

        @pl.when(center)
        def _():
            for which in range(2):
                drain(q2buf.at[q, which], opp_sem.at[q, which])
            left = turn(q2buf[q, 0].reshape(layer_rows, 128))
            right = turn(q2buf[q, 1].reshape(layer_rows, 128))
            far = 2 - 2 * up
            for k in range(blocks):
                grid = dot(left, window(q, far, offset_of(k)))
                grid = grid + dot(right, window(q, far + 1, offset_of(k)))
                sums[k, filt] = sums[k, filt] + folded(grid)

    order = list(range(half, mine)) + list(range(half))
    for q in order:
        start_p(q)
    for q in range(half, mine):
        await_p(q, True)
    for q in range(half, mine):
        start_q(q)
    for q in range(half, mine):
        await_outer(q, True)
    for q in range(half):
        await_p(q, False)
    for q in range(half):
        start_q(q)

    def sent_work(index, carry):
        await_q(half + index)
        own_work(half + index)
        return carry

    def kept_work(q, carry):
        await_outer(q, False)
        await_q(q)
        own_work(q)
        far_work(q)
        return carry

    lax.fori_loop(0, mine - half, sent_work, 0)
    lax.fori_loop(0, half, kept_work, 0)

    rolled = sums[...].reshape(blocks * mine * 8, 128)
    small = lax.broadcasted_iota(jnp.int32, rolled.shape, 0)
    for bit in (1, 2, 4):
        rolled = jnp.where((small & bit) != 0, pltpu.roll(rolled, 128 - bit, 1), rolled)
    summed = jnp.sum(rolled.reshape(blocks * mine, 8, 128), axis=1)
    flip = (128 - col) % 128
    order_mat = (row == jnp.where(up == 1, col, flip)).astype(jnp.float32)
    summed = jnp.dot(
        summed, order_mat, precision=lax.Precision.HIGHEST, preferred_element_type=jnp.float32
    )
    for k in range(blocks):
        lags[k] = summed[k * mine : (k + 1) * mine]

    def first_row(at):
        return jnp.minimum((at * piece) // 128, blocks - 2)

    def hand_out(step, carry):
        to = (me + step) % total
        pltpu.make_async_remote_copy(
            src_ref=lags.at[pl.ds(first_row(to // ch_count), 2)],
            dst_ref=parts.at[me],
            send_sem=xsend,
            recv_sem=xrecv,
            device_id=(to // ch_count, to % ch_count),
            device_id_type=MESH,
        ).start()
        return carry

    lax.fori_loop(1, total, hand_out, 0)
    start_row = first_row(ctx)
    parts[me] = lags[pl.ds(start_row, 2)]
    drain(parts.at[pl.ds(0, total - 1)], xrecv)
    for at in range(depth):
        acc = None
        for lay in range(LAYERS):
            for h in range(ch_count):
                term = parts[(lay * depth + at) * ch_count + h]
                acc = term if acc is None else acc + term
        joined[at * mine : (at + 1) * mine, 0:128] = acc[0]
        joined[at * mine : (at + 1) * mine, 128:256] = acc[1]
    skip = ctx * piece - start_row * 128
    out_ref[...] = pltpu.roll(joined[...], lax.rem(256 - skip, 256), 1)[:, :piece]

    drain(parts.at[pl.ds(0, total - 1)], xsend)
    for q in range(mine):
        drain(landed(q, 0, 0, depth - 1), psend.at[q])
        drain(qbuf.at[q, pl.ds(0, depth - 1)], qsend.at[q])

    @pl.when(outer)
    def _():
        for q in range(mine):
            drain(landed(q, 0), fsend.at[q])

    @pl.when(center)
    def _():
        for q in range(half):
            for which in range(2):
                drain(landed(q, 0), osend.at[q, which])


def local(ctx_count, ch_count, saved_input, out_grad, block_offsets, head_len):
    filters, local_ch, tok_dev = saved_input.shape
    tile_count = tok_dev // 128
    rows = tile_count * local_ch
    blocks = block_offsets.shape[0] + 1
    depth = ctx_count // LAYERS
    mine = filters // depth
    half = mine // 2
    copies = 16 // local_ch
    pieces = rows // 16
    groups = 4 * depth * pieces + 4
    piece = blocks * 128 // ctx_count
    total = ctx_count * ch_count
    loss_scale = 1.0 / math.sqrt(tok_dev * ctx_count * local_ch * ch_count)

    def tiled(array):
        split = array.reshape(filters, local_ch, tile_count, 128)
        return jnp.transpose(split, (0, 2, 1, 3)).reshape(filters, pieces, 16, 128)

    bf16, f32 = jnp.bfloat16, jnp.float32
    dma = pltpu.SemaphoreType.DMA
    taps = pl.pallas_call(
        functools.partial(kernel, ctx_count, ch_count, copies),
        out_shape=jax.ShapeDtypeStruct((filters, piece), f32),
        in_specs=[pl.BlockSpec(memory_space=pltpu.SMEM)] + [pl.BlockSpec(memory_space=pl.ANY)] * 2,
        out_specs=pl.BlockSpec(memory_space=pltpu.VMEM),
        scratch_shapes=[
            pltpu.VMEM((mine, groups, 16, 128), bf16),
            pltpu.VMEM((mine, depth, pieces, 16, 128), bf16),
            pltpu.VMEM((half, 2, depth * pieces, 16, 128), bf16),
            pltpu.VMEM((copies * groups, 16, 128), bf16),
            pltpu.VMEM((blocks, mine, 8, 128), f32),
            pltpu.VMEM((blocks, mine, 128), f32),
            pltpu.VMEM((total, 2, mine, 128), f32),
            pltpu.VMEM((filters, 256), f32),
            dma((2, mine)),
            dma((mine,)),
            dma((mine,)),
            dma((mine,)),
            dma((half, 2)),
            dma((mine,)),
            dma((mine,)),
            dma((mine,)),
            dma((half, 2)),
            dma,
            dma,
        ],
        compiler_params=pltpu.CompilerParams(
            collective_id=0, has_side_effects=True, vmem_limit_bytes=60 * 1024 * 1024
        ),
        cost_estimate=pl.CostEstimate(flops=7 * 10**9, bytes_accessed=4 * 10**6, transcendentals=0),
    )(block_offsets, tiled(saved_input), tiled(out_grad))
    lag = lax.broadcasted_iota(jnp.int32, taps.shape, 1) + lax.axis_index("ctx") * piece
    keep = (lag >= 128) | (lag < head_len[0])
    return jnp.where(keep, taps * loss_scale, jnp.zeros_like(taps))


def solution(mesh):
    ctx_count, ch_count = mesh.shape["ctx"], mesh.shape["ch"]
    in_specs = (P(None, "ch", "ctx"), P(None, "ch", "ctx"), P(), P())
    out_specs = P(None, "ctx")
    return jax.shard_map(
        functools.partial(local, ctx_count, ch_count),
        mesh=mesh, in_specs=in_specs, out_specs=out_specs, check_vma=False,
    )
```
